128 devices in a mesh: bank: 32 (over x, y, core), dp: 4 (over z).
Axes of the slice: x: 4, y: 4, z: 4, core: 2. Of those that a mesh axis runs over, the one named last changes fastest.
Arguments:
- clips: bfloat16 [8192, 256], P(('bank', 'dp')), may hold values from -1 to 1
- queue: bfloat16 [262144, 256], P('bank'), may hold values from -8 to 8
- positive: int32 [8192], P(('bank', 'dp')), may hold values from 0 to 262143, as said below
- cotangent: float32 [8192], P(('bank', 'dp')), may hold values from 0.5 to 12
Outputs:
- clip_grads: float32 [8192, 256], P(('bank', 'dp'))
The draws below stay inside these ranges and needn't reach their ends.
Inputs may be any that keep to these rules, and one draw needn't show every extreme that they name: The clips form 262144 // 8192 equal consecutive groups; the positive of a clip of group g lies among entries g * 8192 to (g + 1) * 8192 - 1.
All inputs are finite; a program needn't handle non-finite values.
Results may differ from the reference program's by a relative error of at most 0.00055.
Values may be sent and summed in bfloat16 or wider, within the bound.
A program may use at most 64 MiB of HBM per device.

```python
import math
import jax
import jax.numpy as jnp
from jax import lax

D = 256
QUEUE_DEV = 8192
CLUSTERS = 2048
QUEUE_ENTRIES = 262144
CLIPS = 8192


def shared_tables(key):
    cluster_of = jax.random.randint(jax.random.fold_in(key, 11), (QUEUE_ENTRIES,), 0, CLUSTERS)
    per_group = CLIPS // (QUEUE_ENTRIES // QUEUE_DEV)
    group_index = jnp.arange(CLIPS, dtype=jnp.int32) // per_group
    offsets = jax.random.randint(jax.random.fold_in(key, 12), (CLIPS,), 0, QUEUE_DEV)
    target = group_index * QUEUE_DEV + offsets
    marked = CLIPS - 1 - jax.random.randint(jax.random.fold_in(key, 13), (), 0, per_group)
    target = jnp.where(jnp.arange(CLIPS, dtype=jnp.int32) == marked, QUEUE_ENTRIES - 1, target)
    centers = jax.random.normal(jax.random.fold_in(key, 14), (CLUSTERS, D), jnp.float32)
    return (cluster_of, target.astype(jnp.int32), centers)


def draw_positive(key, part):
    cluster_of, target, centers = shared_tables(key)
    return target


def draw_queue(key, part):
    cluster_of, target, centers = shared_tables(key)
    key = jax.random.fold_in(key, 3)
    position = jnp.arange(QUEUE_ENTRIES, dtype=jnp.float32) / QUEUE_ENTRIES
    strength = 0.8 + 0.8 * position
    jitter_rows = jax.random.normal(key, (QUEUE_ENTRIES, D), jnp.float32)
    topic_rows = centers[cluster_of] * strength[:, None] + jitter_rows
    return (topic_rows * 0.0625).astype(jnp.bfloat16)


def draw_clips(key, part):
    cluster_of, target, centers = shared_tables(key)
    key = jax.random.fold_in(key, 4)
    topic_rows = centers[cluster_of[target]]
    blend_factor = 1.5
    jitter_rows = jax.random.normal(key, (CLIPS, D), jnp.float32)
    return ((topic_rows * blend_factor + jitter_rows) * 0.00625).astype(jnp.bfloat16)


def draw_cotangent(key, part):
    key = jax.random.fold_in(key, 5)
    position = jnp.arange(CLIPS, dtype=jnp.float32) / max(CLIPS - 1, 1)
    jitter = jax.random.uniform(key, (CLIPS,), jnp.float32, 0.7, 1.3)
    rising = 1.0 + 2.0 * position
    return (rising * jitter).astype(jnp.float32)


def setup_inputs(seed: int = 0) -> dict:
    key_list = jax.random.split(jax.random.key(seed), 5)
    clips = draw_clips(jax.random.fold_in(key_list[4], 71), 0)
    queue = draw_queue(jax.random.fold_in(key_list[4], 71), 0)
    positive = draw_positive(jax.random.fold_in(key_list[4], 71), 0)
    cotangent = draw_cotangent(jax.random.fold_in(key_list[4], 71), 0)
    return {"clips": clips, "queue": queue, "positive": positive, "cotangent": cotangent}


logit_sharpness = 1.0 / 0.07
epsilon = 1e-06
clip_scale = 4.0

def inverse_norms(values):
    return lax.rsqrt(lax.optimization_barrier(jnp.sum(values * values, axis=1)) + epsilon)

def reference(clips, queue, positive, cotangent):
    features = clips.astype(jnp.float32)
    clip_inverse = inverse_norms(features)
    unit_vectors = features * clip_inverse[:, None]
    unit_rows = unit_vectors.astype(jnp.bfloat16)
    block_width = min(4096, QUEUE_ENTRIES)
    stacked = queue.reshape(QUEUE_ENTRIES // block_width, block_width, D)
    row_width = min(512, CLIPS)

    def per_rows(row_block):

        def advance(carry, queue_block):
            totals, moments = carry
            reciprocal = inverse_norms(queue_block.astype(jnp.float32))
            similarity_logits = lax.dot_general(row_block, queue_block, (((1,), (1,)), ((), ())), preferred_element_type=jnp.float32)
            logit_power = jnp.exp(similarity_logits * (reciprocal * logit_sharpness)[None, :])
            totals = totals + lax.optimization_barrier(jnp.sum(logit_power, axis=1))
            weights = (logit_power * reciprocal[None, :]).astype(jnp.bfloat16)
            moments = moments + jnp.dot(weights, queue_block, preferred_element_type=jnp.float32)
            return ((totals, moments), None)
        start_carry = (jnp.zeros((row_width,), jnp.float32), jnp.zeros((row_width, D), jnp.float32))
        result, unused = lax.scan(advance, start_carry, stacked)
        return result
    totals, moments = lax.map(per_rows, unit_rows.reshape(CLIPS // row_width, row_width, D))
    totals = totals.reshape(CLIPS)
    moments = moments.reshape(CLIPS, D)
    positive_rows = jnp.take(queue, positive, axis=0).astype(jnp.float32)
    pushed = moments / totals[:, None] - inverse_norms(positive_rows)[:, None] * positive_rows
    tangent = pushed - unit_vectors * lax.optimization_barrier(jnp.sum(unit_vectors * pushed, axis=1, keepdims=True))
    gradient = cotangent[:, None] * tangent * clip_inverse[:, None]
    squares = jnp.sum(gradient * gradient)
    factor = jnp.minimum(1.0, clip_scale * math.sqrt(CLIPS) / jnp.sqrt(squares + epsilon))
    return gradient * factor
```

```python
import math

import jax
import jax.numpy as jnp
from jax import lax
from jax.experimental import pallas as pl
from jax.experimental.pallas import tpu as pltpu
from jax.sharding import PartitionSpec as P

MESH = pl.DeviceIdType.MESH
LOG2E = 1.4426950408889634
SHARP = 1.0 / 0.07
EPS = 1e-6
F32 = jnp.float32
BF16 = jnp.bfloat16

OWN = 64
D = 256
KQ = 8192
CH = 512
PC = OWN + 8
KB = 2048
SK = 512
STEPS = KQ // KB
NCH = 4
PARTS = 4


def inverse_norms(v):
    return lax.rsqrt(jnp.sum(v * v, axis=1, keepdims=True) + EPS)


def kernel(clips_ref, queue_hbm, pos_ref, cot_ref, out_ref,
           q_ref, rec_ref, sc_ref, rows, acc, tacc, mbuf, pbuf, sbuf, abuf, lbuf, bbuf, prow, sq,
           qsem, gs, gr, ps, pr, ms, mr, as_, ar, bs, br, ss, sr):
    bank = lax.axis_index("bank")
    z = lax.axis_index("dp")
    c = lax.rem(bank, 2)
    y = lax.rem(bank // 2, 4)
    x = bank // 8
    a = (1 - c) * y + c * x
    b = (1 - c) * x + c * y
    step_a = 2 + 6 * c
    step_b = 8 - 6 * c
    partner = bank + 1 - 2 * c

    def dev_a(j):
        return (bank + (lax.rem(a + j, 4) - a) * step_a, z)

    def dev_b(j):
        return (bank + (lax.rem(b + j, 4) - b) * step_b, z)

    def remote(src, dst, s, r, dev):
        return pltpu.make_async_remote_copy(
            src_ref=src, dst_ref=dst, send_sem=s, recv_sem=r, device_id=dev, device_id_type=MESH)

    def queue_copy(i):
        part = pl.ds(i * (KQ // PARTS), KQ // PARTS)
        return pltpu.make_async_copy(queue_hbm.at[part], q_ref.at[part], qsem.at[i])

    for i in range(PARTS):
        queue_copy(i).start()

    barrier = pltpu.get_barrier_semaphore()
    peers = [dev_a(j) for j in (1, 2, 3)] + [dev_b(j) for j in (1, 2, 3)]
    far = []
    for dc in range(2):
        for dz in range(4):
            if dc or dz:
                far.append((bank + dc * (1 - 2 * c), lax.rem(z + dz, 4)))
    for dev in peers + far:
        pl.semaphore_signal(barrier, inc=1, device_id=dev, device_id_type=MESH)

    raw = clips_ref[...].astype(F32)
    inv = inverse_norms(raw)
    dirs = raw * inv
    own0 = pl.multiple_of(c * 256, 256)
    rows[0, pl.ds(own0, OWN), :] = dirs.astype(BF16)

    pl.semaphore_wait(barrier, len(peers) + len(far))

    def piece(t, j, n=1):
        return rows.at[t, pl.ds(pl.multiple_of(own0 + j * OWN, OWN), n * OWN)]

    def a_row(t, j):
        return remote(piece(t, 0), piece(t, j), gs.at[t * 4 + j], gr.at[t * 4 + j], dev_a(4 - j))

    def b_row(t):
        return remote(piece(0, 0), piece(t, 0), gs.at[t * 4], gr.at[t * 4], dev_b(4 - t))

    def p_row(t, j, n, i):
        return remote(piece(t, j, n), piece(t, j, n), ps.at[i], pr.at[i], (partner, z))

    def p_wait(t, j, n, i):
        other = rows.at[t, pl.ds(pl.multiple_of((1 - c) * 256 + j * OWN, OWN), n * OWN)]
        remote(other, other, ps.at[i], pr.at[i], (partner, z)).wait_recv()

    for j in (1, 2, 3):
        a_row(0, j).start()
    p_row(0, 0, 1, 4).start()
    for t in (1, 2, 3):
        b_row(t).start()

    eye = lax.broadcasted_iota(jnp.int32, (OWN, OWN), 0) == lax.broadcasted_iota(jnp.int32, (OWN, OWN), 1)
    local = (pos_ref[...] - bank * KQ).astype(F32).reshape(1, OWN)
    local_col = jnp.sum(jnp.where(eye, local, 0.0), axis=1, keepdims=True).astype(jnp.int32)
    prow[...] = jnp.zeros_like(prow)
    ones = jnp.ones((8, D), BF16)

    def prep(k0, n):
        qb = q_ref[pl.ds(k0, n), :]
        qf = qb.astype(F32)
        s2 = qf * qf
        hi = s2.astype(BF16)
        lo = (s2 - hi.astype(F32)).astype(BF16)
        dims = (((1,), (1,)), ((), ()))
        tot = lax.dot_general(ones, hi, dims, preferred_element_type=F32)
        tot = tot + lax.dot_general(ones, lo, dims, preferred_element_type=F32)
        r = lax.rsqrt(tot[0:1, :] + EPS)
        rec_ref[:, pl.ds(k0, n)] = r
        sc_ref[:, pl.ds(k0, n)] = r * (LOG2E * SHARP)
        place = lax.broadcasted_iota(jnp.int32, (OWN, n), 1) + k0
        hot = jnp.where(place == local_col, 1.0, 0.0).astype(BF16)
        prow[...] += jnp.dot(hot, qb, preferred_element_type=F32)

    for i in range(PARTS):
        queue_copy(i).wait()
        size = KQ // PARTS

        def prep_step(k, _, i=i):
            prep(pl.multiple_of(i * size + k * 512, 512), 512)
            return 0

        lax.fori_loop(0, size // 512, prep_step, 0)

    for j in (1, 2, 3):
        a_row(0, j).wait_recv()
    p_row(0, 1, 3, 0).start()
    for t in (1, 2, 3):
        b_row(t).wait_recv()
        for j in (1, 2, 3):
            a_row(t, j).start()
    p_wait(0, 0, 1, 4)
    p_wait(0, 1, 3, 0)

    half = 4 * PC
    mine0 = pl.multiple_of(c * half, half)
    theirs0 = pl.multiple_of((1 - c) * half, half)

    def to_partner(t):
        return remote(mbuf.at[t, pl.ds(theirs0, half)], pbuf.at[t], ms.at[t], mr.at[t], (partner, z))

    def a_sum(t, j):
        return remote(sbuf.at[t, pl.ds(j * PC, PC)], abuf.at[t, pl.ds((j - 1) * PC, PC)],
                      as_.at[t * 4 + j], ar.at[t * 4 + j], dev_a(j))

    def b_sum(t):
        return remote(lbuf.at[t], bbuf.at[t], bs.at[t], br.at[t], dev_b(t))

    def finish_chunk(t):
        for cc in range(2):
            for j in range(4):
                src = (cc * 4 + j) * OWN
                dst = cc * half + j * PC
                mbuf[t, dst:dst + OWN, :] = acc[src:src + OWN, :]
                col = jnp.sum(tacc[src:src + OWN, :], axis=1, keepdims=True)
                row = jnp.sum(jnp.where(eye, col, 0.0), axis=0, keepdims=True)
                mbuf[t, dst + OWN:dst + PC, :] = jnp.zeros((8, D), F32)
                mbuf[t, dst + OWN:dst + PC, 0:OWN] = jnp.broadcast_to(row, (8, OWN))
        to_partner(t).start()

    def level2(t):
        to_partner(t).wait_recv()
        sbuf[t] = mbuf[t, pl.ds(mine0, half), :] + pbuf[t]
        for j in (1, 2, 3):
            a_sum(t, j).start()

    def level3(t):
        for j in (1, 2, 3):
            a_sum(t, j).wait_recv()
        lbuf[t] = (sbuf[t, 0:PC, :] + abuf[t, 0:PC, :]) + (abuf[t, PC:2 * PC, :] + abuf[t, 2 * PC:3 * PC, :])

        @pl.when(t > 0)
        def _():
            b_sum(t).start()

    def compute(t, s):
        k0 = pl.multiple_of(s * KB, KB)
        total = tacc[...]
        rb = rows[t]
        weights = []
        for i in range(KB // SK):
            k = pl.ds(k0 + i * SK, SK)
            logits = lax.dot_general(rb, q_ref[k, :], (((1,), (1,)), ((), ())), preferred_element_type=F32)
            e = jnp.exp2(logits * sc_ref[:, k])
            for l in range(SK // 128):
                total = total + e[:, l * 128:(l + 1) * 128]
            weights.append((e * rec_ref[:, k]).astype(BF16))
        tacc[...] = total
        acc[...] += jnp.dot(jnp.concatenate(weights, axis=1), q_ref[pl.ds(k0, KB), :], preferred_element_type=F32)

    def step(n, _):
        t = n // STEPS
        s = lax.rem(n, STEPS)

        @pl.when(s == 0)
        def _():
            acc[...] = jnp.zeros_like(acc)
            tacc[...] = jnp.zeros_like(tacc)

            @pl.when(t > 0)
            def _():
                p_wait(t, 0, 4, t)

        compute(t, s)

        @pl.when(n == 1)
        def _():
            for t2 in (1, 2, 3):
                for j in (1, 2, 3):
                    a_row(t2, j).wait_recv()
                p_row(t2, 0, 4, t2).start()

        @pl.when((s == 0) & (t > 0))
        def _():
            level2(t - 1)

        @pl.when((s == 2) & (t > 0))
        def _():
            level3(t - 1)

        @pl.when(s == STEPS - 1)
        def _():
            finish_chunk(t)

        return 0

    lax.fori_loop(0, NCH * STEPS, step, 0)
    level2(NCH - 1)
    prows = prow[...]
    pushed_away = inverse_norms(prows) * prows
    level3(NCH - 1)
    own = lbuf[0]
    for t in (1, 2, 3):
        b_sum(t).wait_recv()
        own = own + bbuf[t]
    totals = jnp.sum(jnp.where(eye, own[OWN:OWN + 1, 0:OWN], 0.0), axis=1, keepdims=True)
    pushed = own[0:OWN, :] / totals - pushed_away
    tangent = pushed - dirs * jnp.sum(dirs * pushed, axis=1, keepdims=True)
    cot = jnp.sum(jnp.where(eye, cot_ref[...].reshape(1, OWN), 0.0), axis=1, keepdims=True)
    gradient = cot * tangent * inv

    squares = jnp.broadcast_to(jnp.sum(gradient * gradient, keepdims=True).reshape(1, 1), (8, 128))

    def round_trip(value, first, devices):
        sq[first] = value
        copies = []
        for i, dev in enumerate(devices):
            n = first + 1 + i
            copies.append(remote(sq.at[first], sq.at[n], ss.at[n], sr.at[n], dev))
            copies[-1].start()
        for i, copy in enumerate(copies):
            copy.wait_recv()
            value = value + sq[first + 1 + i]
        return value, copies

    squares, c1 = round_trip(squares, 0, peers[0:3])
    squares, c2 = round_trip(squares, 4, peers[3:6])
    squares, c3 = round_trip(squares, 8, far)
    clip_total = OWN * lax.axis_size("bank") * lax.axis_size("dp")
    factor = jnp.minimum(1.0, (4.0 * math.sqrt(clip_total)) / jnp.sqrt(squares[0:1, 0:1] + EPS))
    out_ref[...] = gradient * factor

    for copy in c1 + c2 + c3:
        copy.wait_send()
    for t in range(4):
        for j in (1, 2, 3):
            a_row(t, j).wait_send()
            a_sum(t, j).wait_send()
        to_partner(t).wait_send()
        if t:
            b_row(t).wait_send()
            b_sum(t).wait_send()
            p_row(t, 0, 4, t).wait_send()
    p_row(0, 0, 1, 4).wait_send()
    p_row(0, 1, 3, 0).wait_send()


def shards(clips, queue, positive, cotangent):
    vmem = pl.BlockSpec(memory_space=pltpu.VMEM)
    dma = pltpu.SemaphoreType.DMA
    return pl.pallas_call(
        kernel,
        out_shape=jax.ShapeDtypeStruct((OWN, D), F32),
        in_specs=[vmem, pl.BlockSpec(memory_space=pl.ANY), vmem, vmem],
        out_specs=vmem,
        scratch_shapes=[
            pltpu.VMEM((KQ, D), BF16),
            pltpu.VMEM((1, KQ), F32),
            pltpu.VMEM((1, KQ), F32),
            pltpu.VMEM((NCH, CH, D), BF16),
            pltpu.VMEM((CH, D), F32),
            pltpu.VMEM((CH, 128), F32),
            pltpu.VMEM((NCH, 8 * PC, D), F32),
            pltpu.VMEM((NCH, 4 * PC, D), F32),
            pltpu.VMEM((NCH, 4 * PC, D), F32),
            pltpu.VMEM((NCH, 3 * PC, D), F32),
            pltpu.VMEM((NCH, PC, D), F32),
            pltpu.VMEM((NCH, PC, D), F32),
            pltpu.VMEM((OWN, D), F32),
            pltpu.VMEM((16, 8, 128), F32),
            dma((PARTS,)),
            dma((16,)), dma((16,)),
            dma((5,)), dma((5,)),
            dma((4,)), dma((4,)),
            dma((16,)), dma((16,)),
            dma((4,)), dma((4,)),
            dma((16,)), dma((16,)),
        ],
        compiler_params=pltpu.CompilerParams(
            collective_id=0, has_side_effects=True, vmem_limit_bytes=56 << 20),
        cost_estimate=pl.CostEstimate(flops=17 * 10**9, bytes_accessed=5 * 10**6, transcendentals=17 * 10**6),
    )(clips, queue, positive, cotangent)


def solution(mesh):
    in_specs = (P(("bank", "dp"), None), P("bank", None), P(("bank", "dp")), P(("bank", "dp")))
    return jax.shard_map(shards, mesh=mesh, in_specs=in_specs, out_specs=P(("bank", "dp"), None), check_vma=False)
```

```python
import math

import jax
import jax.numpy as jnp
from jax import lax
from jax.experimental import pallas as pl
from jax.experimental.pallas import tpu as pltpu
from jax.sharding import PartitionSpec as P

MESH = pl.DeviceIdType.MESH
LOG2E = 1.4426950408889634
SHARP = 1.0 / 0.07
EPS = 1e-6
F32 = jnp.float32
BF16 = jnp.bfloat16

OWN = 64
D = 256
KQ = 8192
CH = 512
PC = OWN + 8
KB = 2048
SK = 512
STEPS = KQ // KB
NCH = 4
PARTS = 4


def inverse_norms(v):
    return lax.rsqrt(jnp.sum(v * v, axis=1, keepdims=True) + EPS)


def hops(o):
    return sum(min(v, 4 - v) for v in (o[0] % 4, o[1] % 4, o[3] % 4))


CHUNKS = (
    ((0, 0), (1, 1), (1, 3), (3, 1)),
    ((3, 3), (2, 0), (0, 2), (2, 2)),
    ((2, 1), (2, 3), (1, 2), (3, 2)),
    ((1, 0), (3, 0), (0, 1), (0, 3)),
)
NEAR = [(dx, dy, 0, 0) for dx in (0, 1, 3) for dy in (0, 1, 3) if dx or dy]
COLUMN = [(0, 0, dc, dz) for dc in range(2) for dz in range(4) if dc or dz]
ALL = sorted(
    [(dx, dy, dc, dz) for dx in range(4) for dy in range(4) for dc in range(2) for dz in range(4) if dx or dy or dc or dz],
    key=lambda o: -hops(o))


def kernel(clips_ref, queue_hbm, pos_ref, cot_ref, out_ref,
           q_ref, rec_ref, sc_ref, rows, acc, tacc, mbuf, pbuf, sbuf, abuf, prow, sq,
           qsem, go_near, go_column, gs, gr, ps, pr, ms, mr, as_, ar, ss, sr):
    bank = lax.axis_index("bank")
    z = lax.axis_index("dp")
    c = lax.rem(bank, 2)
    y = lax.rem(bank // 2, 4)
    x = bank // 8

    def device(o):
        dx, dy, dc, dz = o
        bx = lax.rem(x + dx, 4) if dx else x
        by = lax.rem(y + dy, 4) if dy else y
        bc = 1 - c if dc else c
        return ((bx * 4 + by) * 2 + bc, lax.rem(z + dz, 4) if dz else z)

    def chip(t, j, back=False):
        dx, dy = CHUNKS[t][j]
        return device(((4 - dx) % 4, (4 - dy) % 4, 0, 0) if back else (dx, dy, 0, 0))

    def remote(src, dst, s, r, dev):
        return pltpu.make_async_remote_copy(
            src_ref=src, dst_ref=dst, send_sem=s, recv_sem=r, device_id=dev, device_id_type=MESH)

    def queue_copy(i):
        part = pl.ds(i * (KQ // PARTS), KQ // PARTS)
        return pltpu.make_async_copy(queue_hbm.at[part], q_ref.at[part], qsem.at[i])

    barrier = pltpu.get_barrier_semaphore()
    for o in NEAR + COLUMN:
        pl.semaphore_signal(barrier, inc=1, device_id=device(o), device_id_type=MESH)
    for i in range(PARTS):
        queue_copy(i).start()

    raw = clips_ref[...].astype(F32)
    inv = inverse_norms(raw)
    dirs = raw * inv
    own0 = pl.multiple_of(c * 256, 256)
    rows[0, pl.ds(own0, OWN), :] = dirs.astype(BF16)

    pl.semaphore_wait(barrier, len(NEAR) + len(COLUMN))

    def piece(t, j, n=1):
        return rows.at[t, pl.ds(pl.multiple_of(own0 + j * OWN, OWN), n * OWN)]

    def row_copy(t, j):
        return remote(piece(0, 0), piece(t, j), gs.at[t * 4 + j], gr.at[t * 4 + j], chip(t, j, back=True))

    def relay(t, j, n, i):
        return remote(piece(t, j, n), piece(t, j, n), ps.at[i], pr.at[i], device((0, 0, 1, 0)))

    def relay_wait(t, j, n, i):
        other = rows.at[t, pl.ds(pl.multiple_of((1 - c) * 256 + j * OWN, OWN), n * OWN)]
        remote(other, other, ps.at[i], pr.at[i], device((0, 0, 1, 0))).wait_recv()

    for j in (1, 2, 3):
        row_copy(0, j).start()
    relay(0, 0, 1, 4).start()
    for o in NEAR:
        pl.semaphore_signal(go_near, inc=1, device_id=device(o), device_id_type=MESH)

    eye = lax.broadcasted_iota(jnp.int32, (OWN, OWN), 0) == lax.broadcasted_iota(jnp.int32, (OWN, OWN), 1)
    local = (pos_ref[...] - bank * KQ).astype(F32).reshape(1, OWN)
    local_col = jnp.sum(jnp.where(eye, local, 0.0), axis=1, keepdims=True).astype(jnp.int32)
    prow[...] = jnp.zeros_like(prow)
    ones = jnp.ones((8, D), BF16)

    def prep(k0, n):
        qb = q_ref[pl.ds(k0, n), :]
        qf = qb.astype(F32)
        s2 = qf * qf
        hi = s2.astype(BF16)
        lo = (s2 - hi.astype(F32)).astype(BF16)
        dims = (((1,), (1,)), ((), ()))
        tot = lax.dot_general(ones, hi, dims, preferred_element_type=F32)
        tot = tot + lax.dot_general(ones, lo, dims, preferred_element_type=F32)
        r = lax.rsqrt(tot[0:1, :] + EPS)
        rec_ref[:, pl.ds(k0, n)] = r
        sc_ref[:, pl.ds(k0, n)] = r * (LOG2E * SHARP)
        place = lax.broadcasted_iota(jnp.int32, (OWN, n), 1) + k0
        hot = jnp.where(place == local_col, 1.0, 0.0).astype(BF16)
        prow[...] += jnp.dot(hot, qb, preferred_element_type=F32)

    def prep_part(i):
        queue_copy(i).wait()
        size = KQ // PARTS

        def prep_step(k, _):
            prep(pl.multiple_of(i * size + k * 512, 512), 512)
            return 0

        lax.fori_loop(0, size // 512, prep_step, 0)

    for i in range(PARTS):
        prep_part(i)

    pl.semaphore_wait(go_near, len(NEAR))
    for t in (1, 2, 3):
        for j in range(4):
            row_copy(t, j).start()
    for o in COLUMN:
        pl.semaphore_signal(go_column, inc=1, device_id=device(o), device_id_type=MESH)

    for j in (1, 2, 3):
        row_copy(0, j).wait_recv()
    relay(0, 1, 3, 0).start()
    relay_wait(0, 0, 1, 4)
    relay_wait(0, 1, 3, 0)

    half = 4 * PC
    mine0 = pl.multiple_of(c * half, half)
    theirs0 = pl.multiple_of((1 - c) * half, half)

    def to_partner(t):
        return remote(mbuf.at[t, pl.ds(theirs0, half)], pbuf.at[t], ms.at[t], mr.at[t], device((0, 0, 1, 0)))

    def to_owner(t, j):
        i = t * 4 + j
        return remote(sbuf.at[t, pl.ds(j * PC, PC)], abuf.at[i], as_.at[i], ar.at[i], chip(t, j))

    def finish_chunk(t):
        for cc in range(2):
            for j in range(4):
                src = (cc * 4 + j) * OWN
                dst = cc * half + j * PC
                mbuf[t, dst:dst + OWN, :] = acc[src:src + OWN, :]
                col = jnp.sum(tacc[src:src + OWN, :], axis=1, keepdims=True)
                row = jnp.sum(jnp.where(eye, col, 0.0), axis=0, keepdims=True)
                mbuf[t, dst + OWN:dst + PC, :] = jnp.zeros((8, D), F32)
                mbuf[t, dst + OWN:dst + PC, 0:OWN] = jnp.broadcast_to(row, (8, OWN))
        to_partner(t).start()

    def send_sums(t):
        to_partner(t).wait_recv()
        sbuf[t] = mbuf[t, pl.ds(mine0, half), :] + pbuf[t]
        for j in range(4):
            if t or j:
                to_owner(t, j).start()

    def compute(t, s):
        k0 = pl.multiple_of(s * KB, KB)
        total = tacc[...]
        rb = rows[t]
        weights = []
        for i in range(KB // SK):
            k = pl.ds(k0 + i * SK, SK)
            logits = lax.dot_general(rb, q_ref[k, :], (((1,), (1,)), ((), ())), preferred_element_type=F32)
            e = jnp.exp2(logits * sc_ref[:, k])
            for l in range(SK // 128):
                total = total + e[:, l * 128:(l + 1) * 128]
            weights.append((e * rec_ref[:, k]).astype(BF16))
        tacc[...] = total
        acc[...] += jnp.dot(jnp.concatenate(weights, axis=1), q_ref[pl.ds(k0, KB), :], preferred_element_type=F32)

    def step(n, _):
        t = n // STEPS
        s = lax.rem(n, STEPS)

        @pl.when(s == 0)
        def _():
            acc[...] = jnp.zeros_like(acc)
            tacc[...] = jnp.zeros_like(tacc)

            @pl.when(t > 0)
            def _():
                relay_wait(t, 0, 4, t)

        compute(t, s)

        for t2, after in ((1, 2), (2, 3), (3, 4)):
            @pl.when(n == after)
            def _(t2=t2):
                for j in range(4):
                    row_copy(t2, j).wait_recv()
                relay(t2, 0, 4, t2).start()

        for t2 in range(NCH - 1):
            @pl.when(n == (t2 + 1) * STEPS)
            def _(t2=t2):
                send_sums(t2)

        @pl.when(s == STEPS - 1)
        def _():
            finish_chunk(t)

        return 0

    lax.fori_loop(0, NCH * STEPS, step, 0)
    send_sums(NCH - 1)
    pl.semaphore_wait(go_column, len(COLUMN))
    prows = prow[...]
    pushed_away = inverse_norms(prows) * prows
    cot = jnp.sum(jnp.where(eye, cot_ref[...].reshape(1, OWN), 0.0), axis=1, keepdims=True)
    own = sbuf[0, 0:PC, :]
    for i in range(1, 16):
        to_owner(i // 4, i % 4).wait_recv()
        own = own + abuf[i]
    totals = jnp.sum(jnp.where(eye, own[OWN:OWN + 1, 0:OWN], 0.0), axis=1, keepdims=True)
    pushed = own[0:OWN, :] / totals - pushed_away
    tangent = pushed - dirs * jnp.sum(dirs * pushed, axis=1, keepdims=True)
    gradient = cot * tangent * inv

    squares = jnp.sum(gradient * gradient, axis=0, keepdims=True)
    sq[0] = squares[:, 0:128] + squares[:, 128:256]
    for i, o in enumerate(ALL):
        remote(sq.at[0], sq.at[i + 1], ss, sr, device(o)).start()
    others = sq.at[pl.ds(1, len(ALL))]
    remote(others, others, ss, sr, device((0, 0, 1, 0))).wait()
    squares = jnp.sum(jnp.sum(sq[...], axis=0), axis=1, keepdims=True)
    clip_total = OWN * lax.axis_size("bank") * lax.axis_size("dp")
    factor = jnp.minimum(1.0, (4.0 * math.sqrt(clip_total)) / jnp.sqrt(squares + EPS))
    out_ref[...] = gradient * factor

    for t in range(4):
        to_partner(t).wait_send()
        for j in range(4):
            if t or j:
                row_copy(t, j).wait_send()
                to_owner(t, j).wait_send()
        if t:
            relay(t, 0, 4, t).wait_send()
    relay(0, 0, 1, 4).wait_send()
    relay(0, 1, 3, 0).wait_send()


def shards(clips, queue, positive, cotangent):
    vmem = pl.BlockSpec(memory_space=pltpu.VMEM)
    dma = pltpu.SemaphoreType.DMA
    return pl.pallas_call(
        kernel,
        out_shape=jax.ShapeDtypeStruct((OWN, D), F32),
        in_specs=[vmem, pl.BlockSpec(memory_space=pl.ANY), vmem, vmem],
        out_specs=vmem,
        scratch_shapes=[
            pltpu.VMEM((KQ, D), BF16),
            pltpu.VMEM((1, KQ), F32),
            pltpu.VMEM((1, KQ), F32),
            pltpu.VMEM((NCH, CH, D), BF16),
            pltpu.VMEM((CH, D), F32),
            pltpu.VMEM((CH, 128), F32),
            pltpu.VMEM((NCH, 8 * PC, D), F32),
            pltpu.VMEM((NCH, 4 * PC, D), F32),
            pltpu.VMEM((NCH, 4 * PC, D), F32),
            pltpu.VMEM((16, PC, D), F32),
            pltpu.VMEM((OWN, D), F32),
            pltpu.VMEM((len(ALL) + 1, 1, 128), F32),
            dma((PARTS,)),
            pltpu.SemaphoreType.REGULAR, pltpu.SemaphoreType.REGULAR,
            dma((16,)), dma((16,)),
            dma((5,)), dma((5,)),
            dma((4,)), dma((4,)),
            dma((16,)), dma((16,)),
            dma, dma,
        ],
        compiler_params=pltpu.CompilerParams(
            collective_id=0, has_side_effects=True, vmem_limit_bytes=56 << 20),
        cost_estimate=pl.CostEstimate(flops=17 * 10**9, bytes_accessed=5 * 10**6, transcendentals=17 * 10**6),
    )(clips, queue, positive, cotangent)


def solution(mesh):
    in_specs = (P(("bank", "dp"), None), P("bank", None), P(("bank", "dp")), P(("bank", "dp")))
    return jax.shard_map(shards, mesh=mesh, in_specs=in_specs, out_specs=P(("bank", "dp"), None), check_vma=False)
```

```python
import math

import jax
import jax.numpy as jnp
from jax import lax
from jax.experimental import pallas as pl
from jax.experimental.pallas import tpu as pltpu
from jax.sharding import PartitionSpec as P

MESH = pl.DeviceIdType.MESH
LOG2E = 1.4426950408889634
SHARP = 1.0 / 0.07
EPS = 1e-6
F32 = jnp.float32
BF16 = jnp.bfloat16

OWN = 64
D = 256
KQ = 8192
CH = 512
PC = OWN + 8
NCH = 4
UNIT = 256
UNITS = CH // UNIT * (KQ // UNIT)
LAG_V = 2
LAG_M = 3
NS = 4
NW = 3
PARTS = 4


def inverse_norms(v):
    return lax.rsqrt(jnp.sum(v * v, axis=1, keepdims=True) + EPS)


def hops(o):
    return sum(min(v, 4 - v) for v in (o[0] % 4, o[1] % 4, o[3] % 4))


CHUNKS = (
    ((0, 0), (1, 1), (1, 3), (3, 1)),
    ((3, 3), (2, 0), (0, 2), (2, 2)),
    ((2, 1), (2, 3), (1, 2), (3, 2)),
    ((1, 0), (3, 0), (0, 1), (0, 3)),
)
NEAR = [(dx, dy, 0, 0) for dx in (0, 1, 3) for dy in (0, 1, 3) if dx or dy]
COLUMN = [(0, 0, dc, dz) for dc in range(2) for dz in range(4) if dc or dz]
ALL = sorted(
    [(dx, dy, dc, dz) for dx in range(4) for dy in range(4) for dc in range(2) for dz in range(4) if dx or dy or dc or dz],
    key=lambda o: -hops(o))


def kernel(clips_ref, queue_hbm, pos_ref, cot_ref, out_ref,
           q_ref, rec_ref, sc_ref, rows, wbuf, tacc, mbuf, pbuf, sbuf, abuf, prow, sq,
           qsem, go_near, go_column, gs, gr, ps, pr, ms, mr, as_, ar, ss, sr):
    bank = lax.axis_index("bank")
    z = lax.axis_index("dp")
    c = lax.rem(bank, 2)
    y = lax.rem(bank // 2, 4)
    x = bank // 8

    def device(o):
        dx, dy, dc, dz = o
        bx = lax.rem(x + dx, 4) if dx else x
        by = lax.rem(y + dy, 4) if dy else y
        bc = 1 - c if dc else c
        return ((bx * 4 + by) * 2 + bc, lax.rem(z + dz, 4) if dz else z)

    def chip(t, j, back=False):
        dx, dy = CHUNKS[t][j]
        return device(((4 - dx) % 4, (4 - dy) % 4, 0, 0) if back else (dx, dy, 0, 0))

    def remote(src, dst, s, r, dev):
        return pltpu.make_async_remote_copy(
            src_ref=src, dst_ref=dst, send_sem=s, recv_sem=r, device_id=dev, device_id_type=MESH)

    def queue_copy(i):
        part = pl.ds(i * (KQ // PARTS), KQ // PARTS)
        return pltpu.make_async_copy(queue_hbm.at[part], q_ref.at[part], qsem.at[i])

    barrier = pltpu.get_barrier_semaphore()
    for o in NEAR + COLUMN:
        pl.semaphore_signal(barrier, inc=1, device_id=device(o), device_id_type=MESH)
    for i in range(PARTS):
        queue_copy(i).start()

    raw = clips_ref[...].astype(F32)
    inv = inverse_norms(raw)
    dirs = raw * inv
    own0 = pl.multiple_of(c * 256, 256)
    rows[0, pl.ds(own0, OWN), :] = dirs.astype(BF16)

    pl.semaphore_wait(barrier, len(NEAR) + len(COLUMN))

    def piece(t, j, n=1):
        return rows.at[t, pl.ds(pl.multiple_of(own0 + j * OWN, OWN), n * OWN)]

    def row_copy(t, j):
        return remote(piece(0, 0), piece(t, j), gs.at[t * 4 + j], gr.at[t * 4 + j], chip(t, j, back=True))

    def relay(t, j, n, i):
        return remote(piece(t, j, n), piece(t, j, n), ps.at[i], pr.at[i], device((0, 0, 1, 0)))

    def relay_wait(t, j, n, i):
        other = rows.at[t, pl.ds(pl.multiple_of((1 - c) * 256 + j * OWN, OWN), n * OWN)]
        remote(other, other, ps.at[i], pr.at[i], device((0, 0, 1, 0))).wait_recv()

    for j in (1, 2, 3):
        row_copy(0, j).start()
    relay(0, 0, 1, 4).start()
    for o in NEAR:
        pl.semaphore_signal(go_near, inc=1, device_id=device(o), device_id_type=MESH)

    eye = lax.broadcasted_iota(jnp.int32, (OWN, OWN), 0) == lax.broadcasted_iota(jnp.int32, (OWN, OWN), 1)
    local = (pos_ref[...] - bank * KQ).astype(F32).reshape(1, OWN)
    local_col = jnp.sum(jnp.where(eye, local, 0.0), axis=1, keepdims=True).astype(jnp.int32)
    ones = jnp.ones((16, D), BF16)

    def prep_tile(k0, i, norms, picked):
        k = pl.ds(pl.multiple_of(k0 + i * UNIT, UNIT), UNIT)
        qb = q_ref[k, :]
        qf = qb.astype(F32)
        s2 = qf * qf
        hi = s2.astype(BF16)
        lo = (s2 - hi.astype(F32)).astype(BF16)
        place = lax.broadcasted_iota(jnp.int32, (OWN, UNIT), 1) + (k0 + i * UNIT)
        hot = jnp.where(place == local_col, 1.0, 0.0).astype(BF16)
        for m, part in ((0, hi), (1, lo)):
            pltpu.matmul_push_rhs(part, 0, m, transpose=True)
            pltpu.matmul_acc_lhs(norms[m][i % 2], ones, load_staged_rhs=0)
        pltpu.matmul_push_rhs(qb, 1, i % 2)
        pltpu.matmul_acc_lhs(picked[i % 2], hot, load_staged_rhs=1)
        total = pltpu.matmul_pop(norms[0][i % 2]) + pltpu.matmul_pop(norms[1][i % 2])
        r = lax.rsqrt(total[0:1, :] + EPS)
        rec_ref[:, k] = r
        sc_ref[:, k] = r * (LOG2E * SHARP)

    def prep(n0, n1, p0, p1):
        size = KQ // PARTS

        def part(p, _):
            queue_copy(p).wait()
            for i in range(size // UNIT):
                prep_tile(p * size, i, (n0, n1), (p0, p1))
            return 0

        lax.fori_loop(0, PARTS, part, 0)
        prow[...] = pltpu.matmul_pop(p0) + pltpu.matmul_pop(p1)

    def two_norms(m):
        return [pltpu.ACC(m)((16, D), F32)] * 2

    pl.run_scoped(prep, two_norms(0), two_norms(1), pltpu.ACC(0)((OWN, D), F32), pltpu.ACC(1)((OWN, D), F32))

    pl.semaphore_wait(go_near, len(NEAR))
    for t in (1, 2, 3):
        for j in range(4):
            row_copy(t, j).start()
    for o in COLUMN:
        pl.semaphore_signal(go_column, inc=1, device_id=device(o), device_id_type=MESH)

    for j in (1, 2, 3):
        row_copy(0, j).wait_recv()
    relay(0, 1, 3, 0).start()
    relay_wait(0, 0, 1, 4)
    relay_wait(0, 1, 3, 0)

    half = 4 * PC
    mine0 = pl.multiple_of(c * half, half)
    theirs0 = pl.multiple_of((1 - c) * half, half)

    def to_partner(t):
        return remote(mbuf.at[t, pl.ds(theirs0, half)], pbuf.at[t], ms.at[t], mr.at[t], device((0, 0, 1, 0)))

    def to_owner(t, j):
        i = t * 4 + j
        return remote(sbuf.at[t, pl.ds(j * PC, PC)], abuf.at[i], as_.at[i], ar.at[i], chip(t, j))

    def finish_chunk(t, moments):
        for cc in range(2):
            popped = pltpu.matmul_pop(moments[cc])
            for j in range(4):
                dst = cc * half + j * PC
                mbuf[t, dst:dst + OWN, :] = popped[j * OWN:(j + 1) * OWN, :]
                src = (cc * 4 + j) * OWN
                col = jnp.sum(tacc[src:src + OWN, :], axis=1, keepdims=True)
                row = jnp.sum(jnp.where(eye, col, 0.0), axis=0, keepdims=True)
                mbuf[t, dst + OWN:dst + PC, :] = jnp.zeros((8, D), F32)
                mbuf[t, dst + OWN:dst + PC, 0:OWN] = jnp.broadcast_to(row, (8, OWN))
        to_partner(t).start()

    def send_sums(t):
        to_partner(t).wait_recv()
        sbuf[t] = mbuf[t, pl.ds(mine0, half), :] + pbuf[t]
        for t2 in range(NCH):
            @pl.when(t == t2)
            def _(t2=t2):
                for j in range(4):
                    if t2 or j:
                        to_owner(t2, j).start()

    def chunk(t, scores, moments):
        tacc[...] = jnp.zeros_like(tacc)

        def entries(u):
            return pl.ds(u // 2 * UNIT, UNIT)

        def start_scores(u):
            part, stage = u % 2, u // 2 % 2
            if part == 0:
                pltpu.matmul_push_rhs(q_ref[entries(u), :], stage, 0, transpose=True)
            pltpu.matmul_acc_lhs(scores[u % len(scores)], rows[t, part * UNIT:(part + 1) * UNIT, :],
                                 load_staged_rhs=stage if part == 0 else None)

        def exponential(u):
            r = slice(u % 2 * UNIT, (u % 2 + 1) * UNIT)
            e = jnp.exp2(pltpu.matmul_pop(scores[u % len(scores)]) * sc_ref[:, entries(u)])
            tacc[r, :] = tacc[r, :] + (e[:, 0:128] + e[:, 128:256])
            wbuf[u % NW] = (e * rec_ref[:, entries(u)]).astype(BF16)

        def start_moments(u):
            part, stage = u % 2, u // 2 % 2
            if part == 0:
                pltpu.matmul_push_rhs(q_ref[entries(u), :], stage, 1)
            pltpu.matmul_acc_lhs(moments[part], wbuf[u % NW], load_staged_rhs=stage if part == 0 else None)

        for s in range(UNITS + LAG_M):
            if s < UNITS:
                start_scores(s)
            if 0 <= s - LAG_V < UNITS:
                exponential(s - LAG_V)
            if 0 <= s - LAG_M:
                start_moments(s - LAG_M)
            if s == 16:
                @pl.when(t > 0)
                def _():
                    send_sums(t - 1)
            if s == 56:
                @pl.when(t == 0)
                def _():
                    pass_on(1)
            if s == 28:
                @pl.when(t == 1)
                def _():
                    pass_on(2)
                    pass_on(3)

        finish_chunk(t, moments)

    def pass_on(t):
        for j in range(4):
            row_copy(t, j).wait_recv()
        relay(t, 0, 4, t).start()

    def chunks(*accumulators):
        def body(t, _):
            @pl.when(t > 0)
            def _():
                relay_wait(t, 0, 4, t)

            chunk(t, accumulators[:NS], accumulators[NS:])
            return 0

        lax.fori_loop(0, NCH, body, 0)

    pl.run_scoped(chunks, *[pltpu.ACC(0)((UNIT, D), F32)] * NS, *[pltpu.ACC(1)((UNIT, D), F32)] * 2)
    send_sums(NCH - 1)
    pl.semaphore_wait(go_column, len(COLUMN))
    prows = prow[...]
    pushed_away = inverse_norms(prows) * prows
    cot = jnp.sum(jnp.where(eye, cot_ref[...].reshape(1, OWN), 0.0), axis=1, keepdims=True)
    own = sbuf[0, 0:PC, :]
    for i in range(1, 16):
        to_owner(i // 4, i % 4).wait_recv()
        own = own + abuf[i]
    totals = jnp.sum(jnp.where(eye, own[OWN:OWN + 1, 0:OWN], 0.0), axis=1, keepdims=True)
    pushed = own[0:OWN, :] / totals - pushed_away
    tangent = pushed - dirs * jnp.sum(dirs * pushed, axis=1, keepdims=True)
    gradient = cot * tangent * inv

    squares = jnp.sum(gradient * gradient, axis=0, keepdims=True)
    sq[0] = squares[:, 0:128] + squares[:, 128:256]
    for i, o in enumerate(ALL):
        remote(sq.at[0], sq.at[i + 1], ss, sr, device(o)).start()
    others = sq.at[pl.ds(1, len(ALL))]
    remote(others, others, ss, sr, device((0, 0, 1, 0))).wait()
    squares = jnp.sum(jnp.sum(sq[...], axis=0), axis=1, keepdims=True)
    clip_total = OWN * lax.axis_size("bank") * lax.axis_size("dp")
    factor = jnp.minimum(1.0, (4.0 * math.sqrt(clip_total)) / jnp.sqrt(squares + EPS))
    out_ref[...] = gradient * factor

    for t in range(4):
        to_partner(t).wait_send()
        for j in range(4):
            if t or j:
                row_copy(t, j).wait_send()
                to_owner(t, j).wait_send()
        if t:
            relay(t, 0, 4, t).wait_send()
    relay(0, 0, 1, 4).wait_send()
    relay(0, 1, 3, 0).wait_send()


def shards(clips, queue, positive, cotangent):
    vmem = pl.BlockSpec(memory_space=pltpu.VMEM)
    dma = pltpu.SemaphoreType.DMA
    return pl.pallas_call(
        kernel,
        out_shape=jax.ShapeDtypeStruct((OWN, D), F32),
        in_specs=[vmem, pl.BlockSpec(memory_space=pl.ANY), vmem, vmem],
        out_specs=vmem,
        scratch_shapes=[
            pltpu.VMEM((KQ, D), BF16),
            pltpu.VMEM((1, KQ), F32),
            pltpu.VMEM((1, KQ), F32),
            pltpu.VMEM((NCH, CH, D), BF16),
            pltpu.VMEM((NW, UNIT, UNIT), BF16),
            pltpu.VMEM((CH, 128), F32),
            pltpu.VMEM((NCH, 8 * PC, D), F32),
            pltpu.VMEM((NCH, 4 * PC, D), F32),
            pltpu.VMEM((NCH, 4 * PC, D), F32),
            pltpu.VMEM((16, PC, D), F32),
            pltpu.VMEM((OWN, D), F32),
            pltpu.VMEM((len(ALL) + 1, 1, 128), F32),
            dma((PARTS,)),
            pltpu.SemaphoreType.REGULAR, pltpu.SemaphoreType.REGULAR,
            dma((16,)), dma((16,)),
            dma((5,)), dma((5,)),
            dma((4,)), dma((4,)),
            dma((16,)), dma((16,)),
            dma, dma,
        ],
        compiler_params=pltpu.CompilerParams(
            collective_id=0, has_side_effects=True, vmem_limit_bytes=56 << 20),
        cost_estimate=pl.CostEstimate(flops=17 * 10**9, bytes_accessed=5 * 10**6, transcendentals=17 * 10**6),
    )(clips, queue, positive, cotangent)


def solution(mesh):
    in_specs = (P(("bank", "dp"), None), P("bank", None), P(("bank", "dp")), P(("bank", "dp")))
    return jax.shard_map(shards, mesh=mesh, in_specs=in_specs, out_specs=P(("bank", "dp"), None), check_vma=False)
```

```python
import math

import jax
import jax.numpy as jnp
from jax import lax
from jax.experimental import pallas as pl
from jax.experimental.pallas import tpu as pltpu
from jax.sharding import PartitionSpec as P

MESH = pl.DeviceIdType.MESH
LOG2E = 1.4426950408889634
SHARP = 1.0 / 0.07
EPS = 1e-6
F32 = jnp.float32
BF16 = jnp.bfloat16

OWN = 64
D = 256
KQ = 8192
CH = 512
PC = OWN + 8
NCH = 4
UNIT = 256
UNITS = CH // UNIT * (KQ // UNIT)
LAG_V = 2
LAG_M = 3
NS = 4
NW = 3
PARTS = 4


def inverse_norms(v):
    return lax.rsqrt(jnp.sum(v * v, axis=1, keepdims=True) + EPS)


def hops(o):
    return sum(min(v, 4 - v) for v in (o[0] % 4, o[1] % 4, o[3] % 4))


CHUNKS = (
    ((0, 0), (2, 0), (0, 2), (3, 3)),
    ((2, 2), (2, 3), (1, 2), (3, 2)),
    ((1, 1), (1, 3), (3, 1), (2, 1)),
    ((1, 0), (3, 0), (0, 1), (0, 3)),
)
NEAR = [(dx, dy, 0, 0) for dx in (0, 1, 3) for dy in (0, 1, 3) if dx or dy] + [(2, 0, 0, 0), (0, 2, 0, 0)]
KNOWN = 0
COLUMN = [(0, 0, dc, dz) for dc in range(2) for dz in range(4) if dc or dz]
ALL = sorted(
    [(dx, dy, dc, dz) for dx in range(4) for dy in range(4) for dc in range(2) for dz in range(4) if dx or dy or dc or dz],
    key=lambda o: -hops(o))


def kernel(clips_hbm, queue_hbm, pos_hbm, cot_hbm, out_ref,
           clips_ref, pos_ref, cot_ref, isem, q_ref, rec_ref, sc_ref, rows, wbuf, tacc, mbuf, pbuf, sbuf, abuf, prow, sq,
           qsem, go_near, go_column, gs, gr, ps, pr, ms, mr, as_, ar, ss, sr):
    bank = lax.axis_index("bank")
    z = lax.axis_index("dp")
    c = lax.rem(bank, 2)
    y = lax.rem(bank // 2, 4)
    x = bank // 8

    at_x = [lax.rem(x + d, 4) * 8 for d in range(4)]
    at_y = [lax.rem(y + d, 4) * 2 for d in range(4)]
    at_c = [c, 1 - c]
    at_z = [lax.rem(z + d, 4) for d in range(4)]

    def device(o):
        dx, dy, dc, dz = o
        return (at_x[dx] + at_y[dy] + at_c[dc], at_z[dz])

    def chip(t, j, back=False):
        dx, dy = CHUNKS[t][j]
        return device(((4 - dx) % 4, (4 - dy) % 4, 0, 0) if back else (dx, dy, 0, 0))

    def remote(src, dst, s, r, dev):
        return pltpu.make_async_remote_copy(
            src_ref=src, dst_ref=dst, send_sem=s, recv_sem=r, device_id=dev, device_id_type=MESH)

    def queue_copy(i):
        part = pl.ds(i * (KQ // PARTS), KQ // PARTS)
        return pltpu.make_async_copy(queue_hbm.at[part], q_ref.at[part], qsem.at[i])

    barrier = pltpu.get_barrier_semaphore()
    for o in NEAR + COLUMN:
        pl.semaphore_signal(barrier, inc=1, device_id=device(o), device_id_type=MESH)
    inputs = [pltpu.make_async_copy(src, dst, isem.at[i])
              for i, (src, dst) in enumerate(((clips_hbm, clips_ref), (pos_hbm, pos_ref), (cot_hbm, cot_ref)))]
    for copy in inputs:
        copy.start()
    for i in range(PARTS):
        queue_copy(i).start()

    inputs[0].wait()
    raw = clips_ref[...].astype(F32)
    inv = inverse_norms(raw)
    dirs = raw * inv
    own0 = pl.multiple_of(c * 256, 256)
    rows[0, pl.ds(own0, OWN), :] = dirs.astype(BF16)

    pl.semaphore_wait(barrier, len(NEAR) + len(COLUMN))

    def piece(t, j, n=1):
        return rows.at[t, pl.ds(pl.multiple_of(own0 + j * OWN, OWN), n * OWN)]

    def row_copy(t, j):
        return remote(piece(0, 0), piece(t, j), gs.at[t * 4 + j], gr.at[t * 4 + j], chip(t, j, back=True))

    def relay(t, j, n, i):
        return remote(piece(t, j, n), piece(t, j, n), ps.at[i], pr.at[i], device((0, 0, 1, 0)))

    def relay_wait(t, j, n, i):
        other = rows.at[t, pl.ds(pl.multiple_of((1 - c) * 256 + j * OWN, OWN), n * OWN)]
        remote(other, other, ps.at[i], pr.at[i], device((0, 0, 1, 0))).wait_recv()

    for j in (1, 2, 3):
        row_copy(0, j).start()
    relay(0, 0, 1, 4).start()
    for j in range(KNOWN):
        row_copy(1, j).start()
    for o in NEAR:
        pl.semaphore_signal(go_near, inc=1, device_id=device(o), device_id_type=MESH)

    inputs[1].wait()
    inputs[2].wait()
    eye = lax.broadcasted_iota(jnp.int32, (OWN, OWN), 0) == lax.broadcasted_iota(jnp.int32, (OWN, OWN), 1)
    local = (pos_ref[...] - bank * KQ).astype(F32).reshape(1, OWN)
    local_col = jnp.sum(jnp.where(eye, local, 0.0), axis=1, keepdims=True).astype(jnp.int32)
    ones = jnp.ones((16, D), BF16)

    def prep_tile(k0, i, norms, picked):
        k = pl.ds(pl.multiple_of(k0 + i * UNIT, UNIT), UNIT)
        qb = q_ref[k, :]
        qf = qb.astype(F32)
        s2 = qf * qf
        hi = s2.astype(BF16)
        lo = (s2 - hi.astype(F32)).astype(BF16)
        place = lax.broadcasted_iota(jnp.int32, (OWN, UNIT), 1) + (k0 + i * UNIT)
        hot = jnp.where(place == local_col, 1.0, 0.0).astype(BF16)
        for m, part in ((0, hi), (1, lo)):
            pltpu.matmul_push_rhs(part, 0, m, transpose=True)
            pltpu.matmul_acc_lhs(norms[m][i % 2], ones, load_staged_rhs=0)
        pltpu.matmul_push_rhs(qb, 1, i % 2)
        pltpu.matmul_acc_lhs(picked[i % 2], hot, load_staged_rhs=1)
        total = pltpu.matmul_pop(norms[0][i % 2]) + pltpu.matmul_pop(norms[1][i % 2])
        r = lax.rsqrt(total[0:1, :] + EPS)
        rec_ref[:, k] = r
        sc_ref[:, k] = r * (LOG2E * SHARP)

    def prep(n0, n1, p0, p1):
        size = KQ // PARTS

        def part(p, _):
            queue_copy(p).wait()
            for i in range(size // UNIT):
                prep_tile(p * size, i, (n0, n1), (p0, p1))
            return 0

        lax.fori_loop(0, PARTS, part, 0)
        prow[...] = pltpu.matmul_pop(p0) + pltpu.matmul_pop(p1)

    def two_norms(m):
        return [pltpu.ACC(m)((16, D), F32)] * 2

    pl.run_scoped(prep, two_norms(0), two_norms(1), pltpu.ACC(0)((OWN, D), F32), pltpu.ACC(1)((OWN, D), F32))

    pl.semaphore_wait(go_near, len(NEAR))
    for j in range(KNOWN, 4):
        row_copy(1, j).start()
    for o in COLUMN:
        pl.semaphore_signal(go_column, inc=1, device_id=device(o), device_id_type=MESH)

    for j in (1, 2, 3):
        row_copy(0, j).wait_recv()
    relay(0, 1, 3, 0).start()
    relay_wait(0, 0, 1, 4)
    relay_wait(0, 1, 3, 0)

    half = 4 * PC
    mine0 = pl.multiple_of(c * half, half)
    theirs0 = pl.multiple_of((1 - c) * half, half)

    def to_partner(t):
        return remote(mbuf.at[t, pl.ds(theirs0, half)], pbuf.at[t], ms.at[t], mr.at[t], device((0, 0, 1, 0)))

    def to_owner(t, j):
        i = t * 4 + j
        return remote(sbuf.at[t, pl.ds(j * PC, PC)], abuf.at[i], as_.at[i], ar.at[i], chip(t, j))

    def finish_chunk(t, moments):
        for cc in range(2):
            popped = pltpu.matmul_pop(moments[cc])
            for j in range(4):
                dst = cc * half + j * PC
                mbuf[t, dst:dst + OWN, :] = popped[j * OWN:(j + 1) * OWN, :]
                src = (cc * 4 + j) * OWN
                col = jnp.sum(tacc[src:src + OWN, :], axis=1, keepdims=True)
                row = jnp.sum(jnp.where(eye, col, 0.0), axis=0, keepdims=True)
                mbuf[t, dst + OWN:dst + PC, :] = jnp.zeros((8, D), F32)
                mbuf[t, dst + OWN:dst + PC, 0:OWN] = jnp.broadcast_to(row, (8, OWN))
        to_partner(t).start()

    def send_sums(t):
        to_partner(t).wait_recv()
        sbuf[t] = mbuf[t, pl.ds(mine0, half), :] + pbuf[t]
        for t2 in range(NCH):
            @pl.when(t == t2)
            def _(t2=t2):
                for j in range(4):
                    if t2 or j:
                        to_owner(t2, j).start()

    def chunk(t, scores, moments):
        tacc[...] = jnp.zeros_like(tacc)

        def entries(u):
            return pl.ds(u // 2 * UNIT, UNIT)

        def start_scores(u):
            part, stage = u % 2, u // 2 % 2
            if part == 0:
                pltpu.matmul_push_rhs(q_ref[entries(u), :], stage, 0, transpose=True)
            pltpu.matmul_acc_lhs(scores[u % len(scores)], rows[t, part * UNIT:(part + 1) * UNIT, :],
                                 load_staged_rhs=stage if part == 0 else None)

        def exponential(u):
            r = slice(u % 2 * UNIT, (u % 2 + 1) * UNIT)
            e = jnp.exp2(pltpu.matmul_pop(scores[u % len(scores)]) * sc_ref[:, entries(u)])
            tacc[r, :] = tacc[r, :] + (e[:, 0:128] + e[:, 128:256])
            wbuf[u % NW] = (e * rec_ref[:, entries(u)]).astype(BF16)

        def start_moments(u):
            part, stage = u % 2, u // 2 % 2
            if part == 0:
                pltpu.matmul_push_rhs(q_ref[entries(u), :], stage, 1)
            pltpu.matmul_acc_lhs(moments[part], wbuf[u % NW], load_staged_rhs=stage if part == 0 else None)

        for s in range(UNITS + LAG_M):
            if s < UNITS:
                start_scores(s)
            if 0 <= s - LAG_V < UNITS:
                exponential(s - LAG_V)
            if 0 <= s - LAG_M:
                start_moments(s - LAG_M)
            if s == 20:
                @pl.when(t > 0)
                def _():
                    send_sums(t - 1)
            if s == 24:
                @pl.when(t == 0)
                def _():
                    for t2 in (2, 3):
                        for j in range(4):
                            row_copy(t2, j).start()
            if s == 62:
                @pl.when(t == 0)
                def _():
                    pass_on(1)
            if s == 36:
                @pl.when(t == 1)
                def _():
                    pass_on(2)

                @pl.when(t == 2)
                def _():
                    pass_on(3)

        finish_chunk(t, moments)

    def pass_on(t):
        for j in range(4):
            row_copy(t, j).wait_recv()
        relay(t, 0, 4, t).start()

    def chunks(*accumulators):
        def body(t, _):
            @pl.when(t > 0)
            def _():
                relay_wait(t, 0, 4, t)

            chunk(t, accumulators[:NS], accumulators[NS:])
            return 0

        lax.fori_loop(0, NCH, body, 0)

    pl.run_scoped(chunks, *[pltpu.ACC(0)((UNIT, D), F32)] * NS, *[pltpu.ACC(1)((UNIT, D), F32)] * 2)
    send_sums(NCH - 1)
    pl.semaphore_wait(go_column, len(COLUMN))
    prows = prow[...]
    pushed_away = inverse_norms(prows) * prows
    cot = jnp.sum(jnp.where(eye, cot_ref[...].reshape(1, OWN), 0.0), axis=1, keepdims=True)
    own = sbuf[0, 0:PC, :]
    for i in range(1, 16):
        to_owner(i // 4, i % 4).wait_recv()
        own = own + abuf[i]
    totals = jnp.sum(jnp.where(eye, own[OWN:OWN + 1, 0:OWN], 0.0), axis=1, keepdims=True)
    pushed = own[0:OWN, :] / totals - pushed_away
    tangent = pushed - dirs * jnp.sum(dirs * pushed, axis=1, keepdims=True)
    gradient = cot * tangent * inv

    squares = jnp.sum(gradient * gradient, axis=0, keepdims=True)
    sq[0] = squares[:, 0:128] + squares[:, 128:256]
    for i, o in enumerate(ALL):
        remote(sq.at[0], sq.at[i + 1], ss, sr, device(o)).start()
    others = sq.at[pl.ds(1, len(ALL))]
    remote(others, others, ss, sr, device((0, 0, 1, 0))).wait()
    squares = jnp.sum(jnp.sum(sq[...], axis=0), axis=1, keepdims=True)
    clip_total = OWN * lax.axis_size("bank") * lax.axis_size("dp")
    factor = jnp.minimum(1.0, (4.0 * math.sqrt(clip_total)) / jnp.sqrt(squares + EPS))
    out_ref[...] = gradient * factor

    for t in range(4):
        to_partner(t).wait_send()
        for j in range(4):
            if t or j:
                row_copy(t, j).wait_send()
                to_owner(t, j).wait_send()
        if t:
            relay(t, 0, 4, t).wait_send()
    relay(0, 0, 1, 4).wait_send()
    relay(0, 1, 3, 0).wait_send()


def shards(clips, queue, positive, cotangent):
    vmem = pl.BlockSpec(memory_space=pltpu.VMEM)
    dma = pltpu.SemaphoreType.DMA
    return pl.pallas_call(
        kernel,
        out_shape=pltpu.VMEM((OWN, D), F32),
        in_specs=[pl.BlockSpec(memory_space=pl.ANY)] * 4,
        out_specs=vmem,
        scratch_shapes=[
            pltpu.VMEM((OWN, D), BF16),
            pltpu.VMEM((OWN,), jnp.int32),
            pltpu.VMEM((OWN,), F32),
            dma((3,)),
            pltpu.VMEM((KQ, D), BF16),
            pltpu.VMEM((1, KQ), F32),
            pltpu.VMEM((1, KQ), F32),
            pltpu.VMEM((NCH, CH, D), BF16),
            pltpu.VMEM((NW, UNIT, UNIT), BF16),
            pltpu.VMEM((CH, 128), F32),
            pltpu.VMEM((NCH, 8 * PC, D), F32),
            pltpu.VMEM((NCH, 4 * PC, D), F32),
            pltpu.VMEM((NCH, 4 * PC, D), F32),
            pltpu.VMEM((16, PC, D), F32),
            pltpu.VMEM((OWN, D), F32),
            pltpu.VMEM((len(ALL) + 1, 1, 128), F32),
            dma((PARTS,)),
            pltpu.SemaphoreType.REGULAR, pltpu.SemaphoreType.REGULAR,
            dma((16,)), dma((16,)),
            dma((5,)), dma((5,)),
            dma((4,)), dma((4,)),
            dma((16,)), dma((16,)),
            dma, dma,
        ],
        compiler_params=pltpu.CompilerParams(
            collective_id=0, has_side_effects=True, vmem_limit_bytes=56 << 20),
        cost_estimate=pl.CostEstimate(flops=17 * 10**9, bytes_accessed=5 * 10**6, transcendentals=17 * 10**6),
    )(clips, queue, positive, cotangent)


def solution(mesh):
    in_specs = (P(("bank", "dp"), None), P("bank", None), P(("bank", "dp")), P(("bank", "dp")))
    return jax.shard_map(shards, mesh=mesh, in_specs=in_specs, out_specs=P(("bank", "dp"), None), check_vma=False)
```

```python
import math

import jax
import jax.numpy as jnp
from jax import lax
from jax.experimental import pallas as pl
from jax.experimental.pallas import tpu as pltpu
from jax.sharding import PartitionSpec as P

MESH = pl.DeviceIdType.MESH
LOG2E = 1.4426950408889634
SHARP = 1.0 / 0.07
EPS = 1e-6
F32 = jnp.float32
BF16 = jnp.bfloat16

OWN = 64
D = 256
KQ = 8192
CH = 256
PC = OWN + 8
NCH = 4
UNIT = 256
UNITS = 2 * KQ // UNIT
LAG_V = 2
LAG_M = 3
NS = 4
NW = 3
PARTS = 4


def inverse_norms(v):
    return lax.rsqrt(jnp.sum(v * v, axis=1, keepdims=True) + EPS)


def hops(o):
    return sum(min(v, 4 - v) for v in (o[0] % 4, o[1] % 4, o[3] % 4))


CHUNKS = (
    ((0, 0), (2, 0), (0, 2), (3, 3)),
    ((2, 2), (2, 3), (1, 2), (3, 2)),
    ((1, 1), (1, 3), (3, 1), (2, 1)),
    ((1, 0), (3, 0), (0, 1), (0, 3)),
)
NEAR = [(dx, dy, 0, 0) for dx in (0, 1, 3) for dy in (0, 1, 3) if dx or dy] + [(2, 0, 0, 0), (0, 2, 0, 0)]
SEND_LATER = 24
KNOWN = 0
COLUMN = [(0, 0, dc, dz) for dc in range(2) for dz in range(4) if dc or dz]
ALL = sorted(
    [(dx, dy, dc, dz) for dx in range(4) for dy in range(4) for dc in range(2) for dz in range(4) if dx or dy or dc or dz],
    key=lambda o: -hops(o))


def kernel(clips_hbm, queue_hbm, pos_hbm, cot_hbm, out_ref,
           clips_ref, pos_ref, cot_ref, q_ref, rec_ref, rows, wbuf, tacc, sbuf, abuf, prow, sq,
           isem, qsem, go_near, go_column, qs, qr, ns, nr, gs, gr, as_, ar, ss, sr):
    bank = lax.axis_index("bank")
    z = lax.axis_index("dp")
    c = lax.rem(bank, 2)
    y = lax.rem(bank // 2, 4)
    x = bank // 8

    at_x = [lax.rem(x + d, 4) * 8 for d in range(4)]
    at_y = [lax.rem(y + d, 4) * 2 for d in range(4)]
    at_c = [c, 1 - c]
    at_z = [lax.rem(z + d, 4) for d in range(4)]

    def device(o):
        dx, dy, dc, dz = o
        return (at_x[dx] + at_y[dy] + at_c[dc], at_z[dz])

    def chip(t, j, back=False):
        dx, dy = CHUNKS[t][j]
        return device(((4 - dx) % 4, (4 - dy) % 4, 0, 0) if back else (dx, dy, 0, 0))

    def remote(src, dst, s, r, dev):
        return pltpu.make_async_remote_copy(
            src_ref=src, dst_ref=dst, send_sem=s, recv_sem=r, device_id=dev, device_id_type=MESH)

    def queue_copy(i):
        part = pl.ds(i * (KQ // PARTS), KQ // PARTS)
        return pltpu.make_async_copy(queue_hbm.at[part], q_ref.at[part], qsem.at[i])

    barrier = pltpu.get_barrier_semaphore()
    for o in NEAR + COLUMN:
        pl.semaphore_signal(barrier, inc=1, device_id=device(o), device_id_type=MESH)
    inputs = [pltpu.make_async_copy(src, dst, isem.at[i])
              for i, (src, dst) in enumerate(((clips_hbm, clips_ref), (pos_hbm, pos_ref), (cot_hbm, cot_ref)))]
    for copy in inputs:
        copy.start()
    for i in range(PARTS):
        queue_copy(i).start()

    inputs[0].wait()
    raw = clips_ref[...].astype(F32)
    inv = inverse_norms(raw)
    dirs = raw * inv
    rows[0, 0:OWN, :] = dirs.astype(BF16)

    pl.semaphore_wait(barrier, len(NEAR) + len(COLUMN))

    def row_copy(t, j):
        return remote(rows.at[0, pl.ds(0, OWN)], rows.at[t, pl.ds(j * OWN, OWN)],
                      gs.at[t * 4 + j], gr.at[t * 4 + j], chip(t, j, back=True))

    partner = device((0, 0, 1, 0))

    def queue_to_partner(i):
        size = KQ // PARTS
        return remote(queue_hbm.at[pl.ds(i * size, size)], q_ref.at[pl.ds(KQ + i * size, size)], qs.at[i], qr.at[i], partner)

    def norms_to_partner():
        return remote(rec_ref.at[:, pl.ds(0, KQ)], rec_ref.at[:, pl.ds(KQ, KQ)], ns, nr, partner)

    for j in (1, 2, 3):
        row_copy(0, j).start()
    for j in range(KNOWN):
        row_copy(1, j).start()
    for i in range(PARTS):
        queue_to_partner(i).start()
    for o in NEAR:
        pl.semaphore_signal(go_near, inc=1, device_id=device(o), device_id_type=MESH)

    inputs[1].wait()
    inputs[2].wait()
    eye = lax.broadcasted_iota(jnp.int32, (OWN, OWN), 0) == lax.broadcasted_iota(jnp.int32, (OWN, OWN), 1)
    local = (pos_ref[...] - bank * KQ).astype(F32).reshape(1, OWN)
    local_col = jnp.sum(jnp.where(eye, local, 0.0), axis=1, keepdims=True).astype(jnp.int32)
    ones = jnp.ones((16, D), BF16)

    def prep_tile(k0, i, norms, picked):
        k = pl.ds(pl.multiple_of(k0 + i * UNIT, UNIT), UNIT)
        qb = q_ref[k, :]
        qf = qb.astype(F32)
        s2 = qf * qf
        hi = s2.astype(BF16)
        lo = (s2 - hi.astype(F32)).astype(BF16)
        place = lax.broadcasted_iota(jnp.int32, (OWN, UNIT), 1) + (k0 + i * UNIT)
        hot = jnp.where(place == local_col, 1.0, 0.0).astype(BF16)
        for m, part in ((0, hi), (1, lo)):
            pltpu.matmul_push_rhs(part, 0, m, transpose=True)
            pltpu.matmul_acc_lhs(norms[m][i % 2], ones, load_staged_rhs=0)
        pltpu.matmul_push_rhs(qb, 1, i % 2)
        pltpu.matmul_acc_lhs(picked[i % 2], hot, load_staged_rhs=1)
        total = pltpu.matmul_pop(norms[0][i % 2]) + pltpu.matmul_pop(norms[1][i % 2])
        rec_ref[:, k] = lax.rsqrt(total[0:1, :] + EPS)

    def prep(n0, n1, p0, p1):
        size = KQ // PARTS

        def part(p, _):
            queue_copy(p).wait()
            for i in range(size // UNIT):
                prep_tile(p * size, i, (n0, n1), (p0, p1))
            return 0

        lax.fori_loop(0, PARTS, part, 0)
        prow[...] = pltpu.matmul_pop(p0) + pltpu.matmul_pop(p1)

    def two_norms(m):
        return [pltpu.ACC(m)((16, D), F32)] * 2

    pl.run_scoped(prep, two_norms(0), two_norms(1), pltpu.ACC(0)((OWN, D), F32), pltpu.ACC(1)((OWN, D), F32))

    norms_to_partner().start()

    pl.semaphore_wait(go_near, len(NEAR))
    for j in range(KNOWN, 4):
        row_copy(1, j).start()
    for o in COLUMN:
        pl.semaphore_signal(go_column, inc=1, device_id=device(o), device_id_type=MESH)

    def to_owner(t, j):
        i = t * 4 + j
        return remote(sbuf.at[t, pl.ds(j * PC, PC)], abuf.at[i], as_.at[i], ar.at[i], chip(t, j))

    def finish_chunk(t, moments):
        popped = pltpu.matmul_pop(moments)
        for j in range(4):
            src, dst = j * OWN, j * PC
            sbuf[t, dst:dst + OWN, :] = popped[src:src + OWN, :]
            col = jnp.sum(tacc[src:src + OWN, :], axis=1, keepdims=True)
            row = jnp.sum(jnp.where(eye, col, 0.0), axis=0, keepdims=True)
            sbuf[t, dst + OWN:dst + PC, :] = jnp.zeros((8, D), F32)
            sbuf[t, dst + OWN:dst + PC, 0:OWN] = jnp.broadcast_to(row, (8, OWN))
        for t2 in range(NCH):
            @pl.when(t == t2)
            def _(t2=t2):
                for j in range(4):
                    if t2 or j:
                        to_owner(t2, j).start()

    def chunk(t, scores, moments):
        tacc[...] = jnp.zeros_like(tacc)

        def entries(u):
            return pl.ds(u * UNIT, UNIT)

        def start_scores(u):
            pltpu.matmul_push_rhs(q_ref[entries(u), :], u % 2, 0, transpose=True)
            pltpu.matmul_acc_lhs(scores[u % NS], rows[t], load_staged_rhs=u % 2)

        def exponential(u):
            r = rec_ref[:, entries(u)]
            e = jnp.exp2(pltpu.matmul_pop(scores[u % NS]) * (r * (LOG2E * SHARP)))
            tacc[...] = tacc[...] + (e[:, 0:128] + e[:, 128:256])
            wbuf[u % NW] = (e * r).astype(BF16)

        def start_moments(u):
            pltpu.matmul_push_rhs(q_ref[entries(u), :], u % 2, 1)
            pltpu.matmul_acc_lhs(moments, wbuf[u % NW], load_staged_rhs=u % 2)

        for s in range(UNITS + LAG_M):
            if s == SEND_LATER:
                @pl.when(t == 0)
                def _():
                    for t2 in (2, 3):
                        for j in range(4):
                            row_copy(t2, j).start()
            if s == UNITS // 2:
                @pl.when(t == 0)
                def _():
                    norms_to_partner().wait_recv()
                    for i in range(PARTS // 2):
                        queue_to_partner(i).wait_recv()
            if s == UNITS * 3 // 4:
                @pl.when(t == 0)
                def _():
                    for i in range(PARTS // 2, PARTS):
                        queue_to_partner(i).wait_recv()
            if s < UNITS:
                start_scores(s)
            if 0 <= s - LAG_V < UNITS:
                exponential(s - LAG_V)
            if 0 <= s - LAG_M:
                start_moments(s - LAG_M)

        finish_chunk(t, moments)

    def chunks(*accumulators):
        def body(t, _):
            for t2 in range(NCH):
                @pl.when(t == t2)
                def _(t2=t2):
                    for j in range(4):
                        if t2 or j:
                            row_copy(t2, j).wait_recv()

            chunk(t, accumulators[:NS], accumulators[NS])
            return 0

        lax.fori_loop(0, NCH, body, 0)

    pl.run_scoped(chunks, *[pltpu.ACC(0)((UNIT, D), F32)] * NS, pltpu.ACC(1)((UNIT, D), F32))
    pl.semaphore_wait(go_column, len(COLUMN))
    prows = prow[...]
    pushed_away = inverse_norms(prows) * prows
    cot = jnp.sum(jnp.where(eye, cot_ref[...].reshape(1, OWN), 0.0), axis=1, keepdims=True)
    own = sbuf[0, 0:PC, :]
    for i in range(1, 16):
        to_owner(i // 4, i % 4).wait_recv()
        own = own + abuf[i]
    totals = jnp.sum(jnp.where(eye, own[OWN:OWN + 1, 0:OWN], 0.0), axis=1, keepdims=True)
    pushed = own[0:OWN, :] / totals - pushed_away
    tangent = pushed - dirs * jnp.sum(dirs * pushed, axis=1, keepdims=True)
    gradient = cot * tangent * inv

    squares = jnp.sum(gradient * gradient, axis=0, keepdims=True)
    sq[0] = squares[:, 0:128] + squares[:, 128:256]
    for i, o in enumerate(ALL):
        remote(sq.at[0], sq.at[i + 1], ss, sr, device(o)).start()
    others = sq.at[pl.ds(1, len(ALL))]
    remote(others, others, ss, sr, device((0, 0, 1, 0))).wait()
    squares = jnp.sum(jnp.sum(sq[...], axis=0), axis=1, keepdims=True)
    clip_total = OWN * lax.axis_size("bank") * lax.axis_size("dp")
    factor = jnp.minimum(1.0, (4.0 * math.sqrt(clip_total)) / jnp.sqrt(squares + EPS))
    out_ref[...] = gradient * factor

    for i in range(1, 16):
        row_copy(i // 4, i % 4).wait_send()
        to_owner(i // 4, i % 4).wait_send()
    for i in range(PARTS):
        queue_to_partner(i).wait_send()
    norms_to_partner().wait_send()


def shards(clips, queue, positive, cotangent):
    vmem = pl.BlockSpec(memory_space=pltpu.VMEM)
    dma = pltpu.SemaphoreType.DMA
    return pl.pallas_call(
        kernel,
        out_shape=pltpu.VMEM((OWN, D), F32),
        in_specs=[pl.BlockSpec(memory_space=pl.ANY)] * 4,
        out_specs=vmem,
        scratch_shapes=[
            pltpu.VMEM((OWN, D), BF16),
            pltpu.VMEM((OWN,), jnp.int32),
            pltpu.VMEM((OWN,), F32),
            pltpu.VMEM((2 * KQ, D), BF16),
            pltpu.VMEM((1, 2 * KQ), F32),
            pltpu.VMEM((NCH, CH, D), BF16),
            pltpu.VMEM((NW, UNIT, UNIT), BF16),
            pltpu.VMEM((CH, 128), F32),
            pltpu.VMEM((NCH, 4 * PC, D), F32),
            pltpu.VMEM((16, PC, D), F32),
            pltpu.VMEM((OWN, D), F32),
            pltpu.VMEM((len(ALL) + 1, 1, 128), F32),
            dma((3,)),
            dma((PARTS,)),
            pltpu.SemaphoreType.REGULAR, pltpu.SemaphoreType.REGULAR,
            dma((PARTS,)), dma((PARTS,)),
            dma, dma,
            dma((16,)), dma((16,)),
            dma((16,)), dma((16,)),
            dma, dma,
        ],
        compiler_params=pltpu.CompilerParams(
            collective_id=0, has_side_effects=True, vmem_limit_bytes=56 << 20),
        cost_estimate=pl.CostEstimate(flops=17 * 10**9, bytes_accessed=5 * 10**6, transcendentals=17 * 10**6),
    )(clips, queue, positive, cotangent)


def solution(mesh):
    in_specs = (P(("bank", "dp"), None), P("bank", None), P(("bank", "dp")), P(("bank", "dp")))
    return jax.shard_map(shards, mesh=mesh, in_specs=in_specs, out_specs=P(("bank", "dp"), None), check_vma=False)
```

```python
import math

import jax
import jax.numpy as jnp
from jax import lax
from jax.experimental import pallas as pl
from jax.experimental.pallas import tpu as pltpu
from jax.sharding import PartitionSpec as P

MESH = pl.DeviceIdType.MESH
LOG2E = 1.4426950408889634
SHARP = 1.0 / 0.07
EPS = 1e-6
F32 = jnp.float32
BF16 = jnp.bfloat16

OWN = 64
D = 256
KQ = 8192
CH = 256
PC = OWN + 8
NCH = 4
UNIT = 256
UNITS = 2 * KQ // UNIT
LAG_V = 2
LAG_M = 3
NS = 4
NW = 4
QUEUE_WAITS = {32: (0, 1), 44: (2,), 54: (3,)}
SEND = 6
PARTS = 4


def inverse_norms(v):
    return lax.rsqrt(jnp.sum(v * v, axis=1, keepdims=True) + EPS)


def hops(o):
    return sum(min(v, 4 - v) for v in (o[0] % 4, o[1] % 4, o[3] % 4))


CHUNKS = (
    ((0, 0), (2, 0), (0, 2), (3, 3)),
    ((2, 2), (2, 3), (1, 2), (3, 2)),
    ((1, 1), (1, 3), (3, 1), (2, 1)),
    ((1, 0), (3, 0), (0, 1), (0, 3)),
)
NEAR = [(dx, dy, 0, 0) for dx in (0, 1, 3) for dy in (0, 1, 3) if dx or dy] + [(2, 0, 0, 0), (0, 2, 0, 0)]
SEND_LATER = 24
KNOWN = 0
COLUMN = [(0, 0, dc, dz) for dc in range(2) for dz in range(4) if dc or dz]
ALL = sorted(
    [(dx, dy, dc, dz) for dx in range(4) for dy in range(4) for dc in range(2) for dz in range(4) if dx or dy or dc or dz],
    key=lambda o: -hops(o))


def kernel(clips_hbm, queue_hbm, pos_hbm, cot_hbm, out_ref,
           clips_ref, pos_ref, cot_ref, q_ref, rec_ref, rows, wbuf, tacc, sbuf, abuf, prow, sq,
           isem, qsem, go_near, go_column, qs, qr, ns, nr, gs, gr, as_, ar, ss, sr):
    bank = lax.axis_index("bank")
    z = lax.axis_index("dp")
    c = lax.rem(bank, 2)
    y = lax.rem(bank // 2, 4)
    x = bank // 8

    at_x = [lax.rem(x + d, 4) * 8 for d in range(4)]
    at_y = [lax.rem(y + d, 4) * 2 for d in range(4)]
    at_c = [c, 1 - c]
    at_z = [lax.rem(z + d, 4) for d in range(4)]

    def device(o):
        dx, dy, dc, dz = o
        return (at_x[dx] + at_y[dy] + at_c[dc], at_z[dz])

    def chip(t, j, back=False):
        dx, dy = CHUNKS[t][j]
        return device(((4 - dx) % 4, (4 - dy) % 4, 0, 0) if back else (dx, dy, 0, 0))

    def remote(src, dst, s, r, dev):
        return pltpu.make_async_remote_copy(
            src_ref=src, dst_ref=dst, send_sem=s, recv_sem=r, device_id=dev, device_id_type=MESH)

    def queue_copy(i):
        part = pl.ds(i * (KQ // PARTS), KQ // PARTS)
        return pltpu.make_async_copy(queue_hbm.at[part], q_ref.at[part], qsem.at[i])

    barrier = pltpu.get_barrier_semaphore()
    for o in NEAR + COLUMN:
        pl.semaphore_signal(barrier, inc=1, device_id=device(o), device_id_type=MESH)
    inputs = [pltpu.make_async_copy(src, dst, isem.at[i])
              for i, (src, dst) in enumerate(((clips_hbm, clips_ref), (pos_hbm, pos_ref), (cot_hbm, cot_ref)))]
    for copy in inputs:
        copy.start()
    for i in range(PARTS):
        queue_copy(i).start()

    inputs[0].wait()
    raw = clips_ref[...].astype(F32)
    inv = inverse_norms(raw)
    dirs = raw * inv
    rows[0, 0:OWN, :] = dirs.astype(BF16)

    pl.semaphore_wait(barrier, len(NEAR) + len(COLUMN))

    def row_copy(t, j):
        return remote(rows.at[0, pl.ds(0, OWN)], rows.at[t, pl.ds(j * OWN, OWN)],
                      gs.at[t * 4 + j], gr.at[t * 4 + j], chip(t, j, back=True))

    partner = device((0, 0, 1, 0))

    def queue_to_partner(i):
        size = KQ // PARTS
        return remote(queue_hbm.at[pl.ds(i * size, size)], q_ref.at[pl.ds(KQ + i * size, size)], qs.at[i], qr.at[i], partner)

    def norms_to_partner():
        return remote(rec_ref.at[:, pl.ds(0, KQ)], rec_ref.at[:, pl.ds(KQ, KQ)], ns, nr, partner)

    for j in (1, 2, 3):
        row_copy(0, j).start()
    for j in range(KNOWN):
        row_copy(1, j).start()
    for i in range(PARTS):
        queue_to_partner(i).start()
    for o in NEAR:
        pl.semaphore_signal(go_near, inc=1, device_id=device(o), device_id_type=MESH)

    inputs[1].wait()
    inputs[2].wait()
    eye = lax.broadcasted_iota(jnp.int32, (OWN, OWN), 0) == lax.broadcasted_iota(jnp.int32, (OWN, OWN), 1)
    local = (pos_ref[...] - bank * KQ).astype(F32).reshape(1, OWN)
    local_col = jnp.sum(jnp.where(eye, local, 0.0), axis=1, keepdims=True).astype(jnp.int32)
    ones = jnp.ones((16, D), BF16)

    def prep_tile(k0, i, norms, picked):
        k = pl.ds(pl.multiple_of(k0 + i * UNIT, UNIT), UNIT)
        qb = q_ref[k, :]
        qf = qb.astype(F32)
        s2 = qf * qf
        hi = s2.astype(BF16)
        lo = (s2 - hi.astype(F32)).astype(BF16)
        place = lax.broadcasted_iota(jnp.int32, (OWN, UNIT), 1) + (k0 + i * UNIT)
        hot = jnp.where(place == local_col, 1.0, 0.0).astype(BF16)
        for m, part in ((0, hi), (1, lo)):
            pltpu.matmul_push_rhs(part, 0, m, transpose=True)
            pltpu.matmul_acc_lhs(norms[m][i % 2], ones, load_staged_rhs=0)
        pltpu.matmul_push_rhs(qb, 1, i % 2)
        pltpu.matmul_acc_lhs(picked[i % 2], hot, load_staged_rhs=1)
        total = pltpu.matmul_pop(norms[0][i % 2]) + pltpu.matmul_pop(norms[1][i % 2])
        rec_ref[:, k] = lax.rsqrt(total[0:1, :] + EPS)

    def prep(n0, n1, p0, p1):
        size = KQ // PARTS

        def part(p, _):
            queue_copy(p).wait()
            for i in range(size // UNIT):
                prep_tile(p * size, i, (n0, n1), (p0, p1))
            return 0

        lax.fori_loop(0, PARTS, part, 0)
        prow[...] = pltpu.matmul_pop(p0) + pltpu.matmul_pop(p1)

    def two_norms(m):
        return [pltpu.ACC(m)((16, D), F32)] * 2

    pl.run_scoped(prep, two_norms(0), two_norms(1), pltpu.ACC(0)((OWN, D), F32), pltpu.ACC(1)((OWN, D), F32))

    norms_to_partner().start()

    pl.semaphore_wait(go_near, len(NEAR))
    for j in range(KNOWN, 4):
        row_copy(1, j).start()
    for o in COLUMN:
        pl.semaphore_signal(go_column, inc=1, device_id=device(o), device_id_type=MESH)

    def to_owner(t, j):
        i = t * 4 + j
        return remote(sbuf.at[t, pl.ds(j * PC, PC)], abuf.at[i], as_.at[i], ar.at[i], chip(t, j))

    def finish_chunk(t, slot, moments):
        popped = pltpu.matmul_pop(moments)
        for j in range(4):
            src, dst = j * OWN, j * PC
            sbuf[t, dst:dst + OWN, :] = popped[src:src + OWN, :]
            col = jnp.sum(tacc[slot, src:src + OWN, :], axis=1, keepdims=True)
            row = jnp.sum(jnp.where(eye, col, 0.0), axis=0, keepdims=True)
            sbuf[t, dst + OWN:dst + PC, :] = jnp.zeros((8, D), F32)
            sbuf[t, dst + OWN:dst + PC, 0:OWN] = jnp.broadcast_to(row, (8, OWN))

    def chunks(*accumulators):
        scores, moments = accumulators[:NS], accumulators[NS]
        wbuf[...] = jnp.zeros_like(wbuf)
        tacc[...] = jnp.zeros_like(tacc)

        def entries(t, u):
            if u >= 0:
                return pl.ds(u * UNIT, UNIT)
            return pl.ds(pl.multiple_of(lax.min(t, 1) * (UNITS + u) * UNIT, UNIT), UNIT)

        def start_scores(t, u):
            pltpu.matmul_push_rhs(q_ref[entries(t, u), :], u % 2, 0, transpose=True)
            pltpu.matmul_acc_lhs(scores[u % NS], rows[t], load_staged_rhs=u % 2)

        def exponential(t, u):
            slot = lax.rem(t, 2) if u >= 0 else lax.rem(t + 1, 2)
            r = rec_ref[:, entries(t, u)]
            e = jnp.exp2(pltpu.matmul_pop(scores[u % NS]) * (r * (LOG2E * SHARP)))
            tacc[slot] = tacc[slot] + (e[:, 0:128] + e[:, 128:256])
            wbuf[u % NW] = (e * r).astype(BF16)

        def start_moments(t, u):
            pltpu.matmul_push_rhs(q_ref[entries(t, u), :], u % 2, 1)
            pltpu.matmul_acc_lhs(moments, wbuf[u % NW], load_staged_rhs=u % 2)

        def body(t, _):
            for t2 in range(NCH):
                @pl.when(t == t2)
                def _(t2=t2):
                    for j in range(4):
                        if t2 or j:
                            row_copy(t2, j).wait_recv()

            for s in range(UNITS):
                if s == SEND:
                    for t2 in range(NCH - 1):
                        @pl.when(t == t2 + 1)
                        def _(t2=t2):
                            for j in range(4):
                                if t2 or j:
                                    to_owner(t2, j).start()
                if s == SEND_LATER:
                    @pl.when(t == 0)
                    def _():
                        for t2 in (2, 3):
                            for j in range(4):
                                row_copy(t2, j).start()
                if s in QUEUE_WAITS:
                    @pl.when(t == 0)
                    def _(s=s):
                        if s == UNITS // 2:
                            norms_to_partner().wait_recv()
                        for i in QUEUE_WAITS[s]:
                            queue_to_partner(i).wait_recv()
                start_scores(t, s)
                if s == LAG_V:
                    tacc[lax.rem(t, 2)] = jnp.zeros((CH, 128), F32)
                exponential(t, s - LAG_V)
                start_moments(t, s - LAG_M)
                if s == LAG_M - 1:
                    finish_chunk(lax.max(t - 1, 0), lax.rem(t + 1, 2), moments)
            return 0

        lax.fori_loop(0, NCH, body, 0)
        last = NCH - 1
        for s in range(UNITS, UNITS + LAG_M):
            if s - LAG_V < UNITS:
                exponential(last, s - LAG_V)
            start_moments(last, s - LAG_M)
        finish_chunk(last, last % 2, moments)
        for j in range(4):
            to_owner(last, j).start()

    pl.run_scoped(chunks, *[pltpu.ACC(0)((UNIT, D), F32)] * NS, pltpu.ACC(1)((UNIT, D), F32))
    pl.semaphore_wait(go_column, len(COLUMN))
    prows = prow[...]
    pushed_away = inverse_norms(prows) * prows
    cot = jnp.sum(jnp.where(eye, cot_ref[...].reshape(1, OWN), 0.0), axis=1, keepdims=True)
    own = sbuf[0, 0:PC, :]
    for i in range(1, 16):
        to_owner(i // 4, i % 4).wait_recv()
        own = own + abuf[i]
    totals = jnp.sum(jnp.where(eye, own[OWN:OWN + 1, 0:OWN], 0.0), axis=1, keepdims=True)
    pushed = own[0:OWN, :] / totals - pushed_away
    tangent = pushed - dirs * jnp.sum(dirs * pushed, axis=1, keepdims=True)
    gradient = cot * tangent * inv

    squares = jnp.sum(gradient * gradient, axis=0, keepdims=True)
    sq[0] = squares[:, 0:128] + squares[:, 128:256]
    for i, o in enumerate(ALL):
        remote(sq.at[0], sq.at[i + 1], ss, sr, device(o)).start()
    others = sq.at[pl.ds(1, len(ALL))]
    remote(others, others, ss, sr, device((0, 0, 1, 0))).wait()
    squares = jnp.sum(jnp.sum(sq[...], axis=0), axis=1, keepdims=True)
    clip_total = OWN * lax.axis_size("bank") * lax.axis_size("dp")
    factor = jnp.minimum(1.0, (4.0 * math.sqrt(clip_total)) / jnp.sqrt(squares + EPS))
    out_ref[...] = gradient * factor

    for i in range(1, 16):
        row_copy(i // 4, i % 4).wait_send()
        to_owner(i // 4, i % 4).wait_send()
    for i in range(PARTS):
        queue_to_partner(i).wait_send()
    norms_to_partner().wait_send()


def shards(clips, queue, positive, cotangent):
    vmem = pl.BlockSpec(memory_space=pltpu.VMEM)
    dma = pltpu.SemaphoreType.DMA
    return pl.pallas_call(
        kernel,
        out_shape=pltpu.VMEM((OWN, D), F32),
        in_specs=[pl.BlockSpec(memory_space=pl.ANY)] * 4,
        out_specs=vmem,
        scratch_shapes=[
            pltpu.VMEM((OWN, D), BF16),
            pltpu.VMEM((OWN,), jnp.int32),
            pltpu.VMEM((OWN,), F32),
            pltpu.VMEM((2 * KQ, D), BF16),
            pltpu.VMEM((1, 2 * KQ), F32),
            pltpu.VMEM((NCH, CH, D), BF16),
            pltpu.VMEM((NW, UNIT, UNIT), BF16),
            pltpu.VMEM((2, CH, 128), F32),
            pltpu.VMEM((NCH, 4 * PC, D), F32),
            pltpu.VMEM((16, PC, D), F32),
            pltpu.VMEM((OWN, D), F32),
            pltpu.VMEM((len(ALL) + 1, 1, 128), F32),
            dma((3,)),
            dma((PARTS,)),
            pltpu.SemaphoreType.REGULAR, pltpu.SemaphoreType.REGULAR,
            dma((PARTS,)), dma((PARTS,)),
            dma, dma,
            dma((16,)), dma((16,)),
            dma((16,)), dma((16,)),
            dma, dma,
        ],
        compiler_params=pltpu.CompilerParams(
            collective_id=0, has_side_effects=True, vmem_limit_bytes=56 << 20),
        cost_estimate=pl.CostEstimate(flops=17 * 10**9, bytes_accessed=5 * 10**6, transcendentals=17 * 10**6),
    )(clips, queue, positive, cotangent)


def solution(mesh):
    in_specs = (P(("bank", "dp"), None), P("bank", None), P(("bank", "dp")), P(("bank", "dp")))
    return jax.shard_map(shards, mesh=mesh, in_specs=in_specs, out_specs=P(("bank", "dp"), None), check_vma=False)
```

```python
import math

import jax
import jax.numpy as jnp
from jax import lax
from jax.experimental import pallas as pl
from jax.experimental.pallas import tpu as pltpu
from jax.sharding import PartitionSpec as P

MESH = pl.DeviceIdType.MESH
LOG2E = 1.4426950408889634
SHARP = 1.0 / 0.07
EPS = 1e-6
F32 = jnp.float32
BF16 = jnp.bfloat16

OWN = 64
D = 256
KQ = 8192
CH = 256
NCH = 4
UNIT = 256
UNITS = 2 * KQ // UNIT
LAG_V = 2
LAG_M = 3
NS = 4
NW = 4
QUEUE_WAITS = {32: (0, 1), 44: (2,), 54: (3,)}
SEND = 6
PARTS = 4


def inverse_norms(v):
    return lax.rsqrt(jnp.sum(v * v, axis=1, keepdims=True) + EPS)


def hops(o):
    return sum(min(v, 4 - v) for v in (o[0] % 4, o[1] % 4, o[3] % 4))


CHUNKS = (
    ((0, 0), (2, 0), (0, 2), (3, 3)),
    ((2, 2), (2, 3), (1, 2), (3, 2)),
    ((1, 1), (1, 3), (3, 1), (2, 1)),
    ((1, 0), (3, 0), (0, 1), (0, 3)),
)
NEAR = [(dx, dy, 0, 0) for dx in (0, 1, 3) for dy in (0, 1, 3) if dx or dy] + [(2, 0, 0, 0), (0, 2, 0, 0)]
SEND_LATER = 24
KNOWN = 0
COLUMN = [(0, 0, dc, dz) for dc in range(2) for dz in range(4) if dc or dz]
ALL = sorted(
    [(dx, dy, dc, dz) for dx in range(4) for dy in range(4) for dc in range(2) for dz in range(4) if dx or dy or dc or dz],
    key=lambda o: -hops(o))


def kernel(clips_hbm, queue_hbm, pos_hbm, cot_hbm, out_ref,
           clips_ref, pos_ref, cot_ref, q_ref, rec_ref, rows, wbuf, tacc, sbuf, abuf, tsend, tgot, prow, sq,
           isem, qsem, go_near, go_column, qs, qr, ns, nr, gs, gr, as_, ar, ts, tr, ss, sr):
    bank = lax.axis_index("bank")
    z = lax.axis_index("dp")
    c = lax.rem(bank, 2)
    y = lax.rem(bank // 2, 4)
    x = bank // 8

    at_x = [lax.rem(x + d, 4) * 8 for d in range(4)]
    at_y = [lax.rem(y + d, 4) * 2 for d in range(4)]
    at_c = [c, 1 - c]
    at_z = [lax.rem(z + d, 4) for d in range(4)]

    def device(o):
        dx, dy, dc, dz = o
        return (at_x[dx] + at_y[dy] + at_c[dc], at_z[dz])

    def chip(t, j, back=False):
        dx, dy = CHUNKS[t][j]
        return device(((4 - dx) % 4, (4 - dy) % 4, 0, 0) if back else (dx, dy, 0, 0))

    def remote(src, dst, s, r, dev):
        return pltpu.make_async_remote_copy(
            src_ref=src, dst_ref=dst, send_sem=s, recv_sem=r, device_id=dev, device_id_type=MESH)

    def queue_copy(i):
        part = pl.ds(i * (KQ // PARTS), KQ // PARTS)
        return pltpu.make_async_copy(queue_hbm.at[part], q_ref.at[part], qsem.at[i])

    barrier = pltpu.get_barrier_semaphore()
    for o in NEAR + COLUMN:
        pl.semaphore_signal(barrier, inc=1, device_id=device(o), device_id_type=MESH)
    inputs = [pltpu.make_async_copy(src, dst, isem.at[i])
              for i, (src, dst) in enumerate(((clips_hbm, clips_ref), (pos_hbm, pos_ref), (cot_hbm, cot_ref)))]
    for copy in inputs:
        copy.start()
    for i in range(PARTS):
        queue_copy(i).start()

    inputs[0].wait()
    raw = clips_ref[...].astype(F32)
    inv = inverse_norms(raw)
    dirs = raw * inv
    rows[0, 0:OWN, :] = dirs.astype(BF16)

    pl.semaphore_wait(barrier, len(NEAR) + len(COLUMN))

    def row_copy(t, j):
        return remote(rows.at[0, pl.ds(0, OWN)], rows.at[t, pl.ds(j * OWN, OWN)],
                      gs.at[t * 4 + j], gr.at[t * 4 + j], chip(t, j, back=True))

    partner = device((0, 0, 1, 0))

    def queue_to_partner(i):
        size = KQ // PARTS
        return remote(queue_hbm.at[pl.ds(i * size, size)], q_ref.at[pl.ds(KQ + i * size, size)], qs.at[i], qr.at[i], partner)

    def norms_to_partner():
        return remote(rec_ref.at[:, pl.ds(0, KQ)], rec_ref.at[:, pl.ds(KQ, KQ)], ns, nr, partner)

    for j in (1, 2, 3):
        row_copy(0, j).start()
    for j in range(KNOWN):
        row_copy(1, j).start()
    for i in range(PARTS):
        queue_to_partner(i).start()
    for o in NEAR:
        pl.semaphore_signal(go_near, inc=1, device_id=device(o), device_id_type=MESH)

    inputs[1].wait()
    inputs[2].wait()
    eye = lax.broadcasted_iota(jnp.int32, (OWN, OWN), 0) == lax.broadcasted_iota(jnp.int32, (OWN, OWN), 1)
    wide_eye = lax.broadcasted_iota(jnp.int32, (OWN, 128), 0) == lax.broadcasted_iota(jnp.int32, (OWN, 128), 1)
    local = (pos_ref[...] - bank * KQ).astype(F32).reshape(1, OWN)
    local_col = jnp.sum(jnp.where(eye, local, 0.0), axis=1, keepdims=True).astype(jnp.int32)
    ones = jnp.ones((16, D), BF16)

    def prep_tile(k0, i, norms, picked):
        k = pl.ds(pl.multiple_of(k0 + i * UNIT, UNIT), UNIT)
        qb = q_ref[k, :]
        qf = qb.astype(F32)
        s2 = qf * qf
        hi = s2.astype(BF16)
        lo = (s2 - hi.astype(F32)).astype(BF16)
        place = lax.broadcasted_iota(jnp.int32, (OWN, UNIT), 1) + (k0 + i * UNIT)
        hot = jnp.where(place == local_col, 1.0, 0.0).astype(BF16)
        for m, part in ((0, hi), (1, lo)):
            pltpu.matmul_push_rhs(part, 0, m, transpose=True)
            pltpu.matmul_acc_lhs(norms[m][i % 2], ones, load_staged_rhs=0)
        pltpu.matmul_push_rhs(qb, 1, i % 2)
        pltpu.matmul_acc_lhs(picked[i % 2], hot, load_staged_rhs=1)
        total = pltpu.matmul_pop(norms[0][i % 2]) + pltpu.matmul_pop(norms[1][i % 2])
        rec_ref[:, k] = lax.rsqrt(total[0:1, :] + EPS)

    def prep(n0, n1, p0, p1):
        size = KQ // PARTS

        def part(p, _):
            queue_copy(p).wait()
            for i in range(size // UNIT):
                prep_tile(p * size, i, (n0, n1), (p0, p1))
            return 0

        lax.fori_loop(0, PARTS, part, 0)
        prow[...] = pltpu.matmul_pop(p0) + pltpu.matmul_pop(p1)

    def two_norms(m):
        return [pltpu.ACC(m)((16, D), F32)] * 2

    pl.run_scoped(prep, two_norms(0), two_norms(1), pltpu.ACC(0)((OWN, D), F32), pltpu.ACC(1)((OWN, D), F32))

    norms_to_partner().start()

    pl.semaphore_wait(go_near, len(NEAR))
    for j in range(KNOWN, 4):
        row_copy(1, j).start()
    for o in COLUMN:
        pl.semaphore_signal(go_column, inc=1, device_id=device(o), device_id_type=MESH)

    class to_owner:
        def __init__(self, t, j):
            i = t * 4 + j
            dev = chip(t, j)
            self.copies = (
                remote(tsend.at[i], tgot.at[i], ts.at[i], tr.at[i], dev),
                remote(sbuf.at[t, pl.ds(j * OWN, OWN)], abuf.at[i], as_.at[i], ar.at[i], dev))

        def start(self):
            for copy in self.copies:
                copy.start()

        def wait_recv(self):
            for copy in self.copies:
                copy.wait_recv()

        def wait_send(self):
            for copy in self.copies:
                copy.wait_send()

    def finish_chunk(t, slot, moments):
        sbuf[t] = pltpu.matmul_pop(moments)
        for j in range(4):
            col = jnp.sum(tacc[slot, j * OWN:(j + 1) * OWN, :], axis=1, keepdims=True)
            tsend[t * 4 + j] = jnp.sum(jnp.where(wide_eye, col, 0.0), axis=0, keepdims=True)

    def chunks(*accumulators):
        scores, moments = accumulators[:NS], accumulators[NS]
        wbuf[...] = jnp.zeros_like(wbuf)
        tacc[...] = jnp.zeros_like(tacc)

        def entries(t, u):
            if u >= 0:
                return pl.ds(u * UNIT, UNIT)
            return pl.ds(pl.multiple_of(lax.min(t, 1) * (UNITS + u) * UNIT, UNIT), UNIT)

        def start_scores(t, u):
            pltpu.matmul_push_rhs(q_ref[entries(t, u), :], u % 2, 0, transpose=True)
            pltpu.matmul_acc_lhs(scores[u % NS], rows[t], load_staged_rhs=u % 2)

        def exponential(t, u):
            slot = lax.rem(t, 2) if u >= 0 else lax.rem(t + 1, 2)
            r = rec_ref[:, entries(t, u)]
            e = jnp.exp2(pltpu.matmul_pop(scores[u % NS]) * (r * (LOG2E * SHARP)))
            tacc[slot] = tacc[slot] + (e[:, 0:128] + e[:, 128:256])
            wbuf[u % NW] = (e * r).astype(BF16)

        def start_moments(t, u):
            pltpu.matmul_push_rhs(q_ref[entries(t, u), :], u % 2, 1)
            pltpu.matmul_acc_lhs(moments, wbuf[u % NW], load_staged_rhs=u % 2)

        def body(t, _):
            for t2 in range(NCH):
                @pl.when(t == t2)
                def _(t2=t2):
                    for j in range(4):
                        if t2 or j:
                            row_copy(t2, j).wait_recv()

            for s in range(UNITS):
                if s == SEND:
                    for t2 in range(NCH - 1):
                        @pl.when(t == t2 + 1)
                        def _(t2=t2):
                            for j in range(4):
                                if t2 or j:
                                    to_owner(t2, j).start()
                if s == SEND_LATER:
                    @pl.when(t == 0)
                    def _():
                        for t2 in (2, 3):
                            for j in range(4):
                                row_copy(t2, j).start()
                if s in QUEUE_WAITS:
                    @pl.when(t == 0)
                    def _(s=s):
                        if s == UNITS // 2:
                            norms_to_partner().wait_recv()
                        for i in QUEUE_WAITS[s]:
                            queue_to_partner(i).wait_recv()
                start_scores(t, s)
                if s == LAG_V:
                    tacc[lax.rem(t, 2)] = jnp.zeros((CH, 128), F32)
                exponential(t, s - LAG_V)
                start_moments(t, s - LAG_M)
                if s == LAG_M - 1:
                    finish_chunk(lax.max(t - 1, 0), lax.rem(t + 1, 2), moments)
            return 0

        lax.fori_loop(0, NCH, body, 0)
        last = NCH - 1
        for s in range(UNITS, UNITS + LAG_M):
            if s - LAG_V < UNITS:
                exponential(last, s - LAG_V)
            start_moments(last, s - LAG_M)
        finish_chunk(last, last % 2, moments)
        for j in range(4):
            to_owner(last, j).start()

    pl.run_scoped(chunks, *[pltpu.ACC(0)((UNIT, D), F32)] * NS, pltpu.ACC(1)((UNIT, D), F32))
    pl.semaphore_wait(go_column, len(COLUMN))
    prows = prow[...]
    pushed_away = inverse_norms(prows) * prows
    cot = jnp.sum(jnp.where(eye, cot_ref[...].reshape(1, OWN), 0.0), axis=1, keepdims=True)
    own, own_totals = sbuf[0, 0:OWN, :], tsend[0]
    for i in range(1, 16):
        to_owner(i // 4, i % 4).wait_recv()
        own, own_totals = own + abuf[i], own_totals + tgot[i]
    totals = jnp.sum(jnp.where(wide_eye, own_totals, 0.0), axis=1, keepdims=True)
    pushed = own / totals - pushed_away
    tangent = pushed - dirs * jnp.sum(dirs * pushed, axis=1, keepdims=True)
    gradient = cot * tangent * inv

    squares = jnp.sum(gradient * gradient, axis=0, keepdims=True)
    sq[0] = squares[:, 0:128] + squares[:, 128:256]
    for i, o in enumerate(ALL):
        remote(sq.at[0], sq.at[i + 1], ss, sr, device(o)).start()
    others = sq.at[pl.ds(1, len(ALL))]
    remote(others, others, ss, sr, device((0, 0, 1, 0))).wait()
    squares = jnp.sum(jnp.sum(sq[...], axis=0), axis=1, keepdims=True)
    clip_total = OWN * lax.axis_size("bank") * lax.axis_size("dp")
    factor = jnp.minimum(1.0, (4.0 * math.sqrt(clip_total)) / jnp.sqrt(squares + EPS))
    out_ref[...] = gradient * factor

    for i in range(1, 16):
        row_copy(i // 4, i % 4).wait_send()
        to_owner(i // 4, i % 4).wait_send()
    for i in range(PARTS):
        queue_to_partner(i).wait_send()
    norms_to_partner().wait_send()


def shards(clips, queue, positive, cotangent):
    vmem = pl.BlockSpec(memory_space=pltpu.VMEM)
    dma = pltpu.SemaphoreType.DMA
    return pl.pallas_call(
        kernel,
        out_shape=pltpu.VMEM((OWN, D), F32),
        in_specs=[pl.BlockSpec(memory_space=pl.ANY)] * 4,
        out_specs=vmem,
        scratch_shapes=[
            pltpu.VMEM((OWN, D), BF16),
            pltpu.VMEM((OWN,), jnp.int32),
            pltpu.VMEM((OWN,), F32),
            pltpu.VMEM((2 * KQ, D), BF16),
            pltpu.VMEM((1, 2 * KQ), F32),
            pltpu.VMEM((NCH, CH, D), BF16),
            pltpu.VMEM((NW, UNIT, UNIT), BF16),
            pltpu.VMEM((2, CH, 128), F32),
            pltpu.VMEM((NCH, CH, D), F32),
            pltpu.VMEM((16, OWN, D), F32),
            pltpu.VMEM((16, 1, 128), F32),
            pltpu.VMEM((16, 1, 128), F32),
            pltpu.VMEM((OWN, D), F32),
            pltpu.VMEM((len(ALL) + 1, 1, 128), F32),
            dma((3,)),
            dma((PARTS,)),
            pltpu.SemaphoreType.REGULAR, pltpu.SemaphoreType.REGULAR,
            dma((PARTS,)), dma((PARTS,)),
            dma, dma,
            dma((16,)), dma((16,)),
            dma((16,)), dma((16,)),
            dma((16,)), dma((16,)),
            dma, dma,
        ],
        compiler_params=pltpu.CompilerParams(
            collective_id=0, has_side_effects=True, vmem_limit_bytes=56 << 20),
        cost_estimate=pl.CostEstimate(flops=17 * 10**9, bytes_accessed=5 * 10**6, transcendentals=17 * 10**6),
    )(clips, queue, positive, cotangent)


def solution(mesh):
    in_specs = (P(("bank", "dp"), None), P("bank", None), P(("bank", "dp")), P(("bank", "dp")))
    return jax.shard_map(shards, mesh=mesh, in_specs=in_specs, out_specs=P(("bank", "dp"), None), check_vma=False)
```

```python
import math

import jax
import jax.numpy as jnp
from jax import lax
from jax.experimental import pallas as pl
from jax.experimental.pallas import tpu as pltpu
from jax.sharding import PartitionSpec as P

MESH = pl.DeviceIdType.MESH
LOG2E = 1.4426950408889634
SHARP = 1.0 / 0.07
EPS = 1e-6
F32 = jnp.float32
BF16 = jnp.bfloat16

OWN = 64
D = 256
KQ = 8192
CH = 256
PC = OWN + 8
NCH = 4
UNIT = 256
UNITS = 2 * KQ // UNIT
LAG_V = 3
LAG_M = 4
NS = 4
NW = 4
QUEUE_WAITS = {32: (0, 1), 44: (2,), 54: (3,)}
SEND = 6
PARTS = 4


def inverse_norms(v):
    return lax.rsqrt(jnp.sum(v * v, axis=1, keepdims=True) + EPS)


def hops(o):
    return sum(min(v, 4 - v) for v in (o[0] % 4, o[1] % 4, o[3] % 4))


CHUNKS = (
    ((0, 0), (2, 0), (0, 2), (3, 3)),
    ((2, 2), (2, 3), (1, 2), (3, 2)),
    ((1, 1), (1, 3), (3, 1), (2, 1)),
    ((1, 0), (3, 0), (0, 1), (0, 3)),
)
NEAR = [(dx, dy, 0, 0) for dx in (0, 1, 3) for dy in (0, 1, 3) if dx or dy] + [(2, 0, 0, 0), (0, 2, 0, 0)]
SEND_LATER = 24
KNOWN = 0
COLUMN = [(0, 0, dc, dz) for dc in range(2) for dz in range(4) if dc or dz]
ALL = sorted(
    [(dx, dy, dc, dz) for dx in range(4) for dy in range(4) for dc in range(2) for dz in range(4) if dx or dy or dc or dz],
    key=lambda o: -hops(o))


def kernel(clips_hbm, queue_hbm, pos_hbm, cot_hbm, out_ref,
           clips_ref, pos_ref, cot_ref, q_ref, rec_ref, rows, wbuf, tacc, sbuf, abuf, prow, sq,
           isem, qsem, go_near, go_column, qs, qr, ns, nr, gs, gr, as_, ar, ss, sr):
    bank = lax.axis_index("bank")
    z = lax.axis_index("dp")
    c = lax.rem(bank, 2)
    y = lax.rem(bank // 2, 4)
    x = bank // 8

    at_x = [lax.rem(x + d, 4) * 8 for d in range(4)]
    at_y = [lax.rem(y + d, 4) * 2 for d in range(4)]
    at_c = [c, 1 - c]
    at_z = [lax.rem(z + d, 4) for d in range(4)]

    def device(o):
        dx, dy, dc, dz = o
        return (at_x[dx] + at_y[dy] + at_c[dc], at_z[dz])

    def chip(t, j, back=False):
        dx, dy = CHUNKS[t][j]
        return device(((4 - dx) % 4, (4 - dy) % 4, 0, 0) if back else (dx, dy, 0, 0))

    def remote(src, dst, s, r, dev):
        return pltpu.make_async_remote_copy(
            src_ref=src, dst_ref=dst, send_sem=s, recv_sem=r, device_id=dev, device_id_type=MESH)

    def queue_copy(i):
        part = pl.ds(i * (KQ // PARTS), KQ // PARTS)
        return pltpu.make_async_copy(queue_hbm.at[part], q_ref.at[part], qsem.at[i])

    barrier = pltpu.get_barrier_semaphore()
    for o in NEAR + COLUMN:
        pl.semaphore_signal(barrier, inc=1, device_id=device(o), device_id_type=MESH)
    inputs = [pltpu.make_async_copy(src, dst, isem.at[i])
              for i, (src, dst) in enumerate(((clips_hbm, clips_ref), (pos_hbm, pos_ref), (cot_hbm, cot_ref)))]
    for copy in inputs:
        copy.start()
    for i in range(PARTS):
        queue_copy(i).start()

    inputs[0].wait()
    raw = clips_ref[...].astype(F32)
    inv = inverse_norms(raw)
    dirs = raw * inv
    rows[0, 0:OWN, :] = dirs.astype(BF16)

    pl.semaphore_wait(barrier, len(NEAR) + len(COLUMN))

    def row_copy(t, j):
        return remote(rows.at[0, pl.ds(0, OWN)], rows.at[t, pl.ds(j * OWN, OWN)],
                      gs.at[t * 4 + j], gr.at[t * 4 + j], chip(t, j, back=True))

    partner = device((0, 0, 1, 0))

    def queue_to_partner(i):
        size = KQ // PARTS
        return remote(queue_hbm.at[pl.ds(i * size, size)], q_ref.at[pl.ds(KQ + i * size, size)], qs.at[i], qr.at[i], partner)

    def norms_to_partner():
        return remote(rec_ref.at[:, pl.ds(0, KQ)], rec_ref.at[:, pl.ds(KQ, KQ)], ns, nr, partner)

    for j in (1, 2, 3):
        row_copy(0, j).start()
    for j in range(KNOWN):
        row_copy(1, j).start()
    for i in range(PARTS):
        queue_to_partner(i).start()
    for o in NEAR:
        pl.semaphore_signal(go_near, inc=1, device_id=device(o), device_id_type=MESH)

    inputs[1].wait()
    inputs[2].wait()
    eye = lax.broadcasted_iota(jnp.int32, (OWN, OWN), 0) == lax.broadcasted_iota(jnp.int32, (OWN, OWN), 1)
    local = (pos_ref[...] - bank * KQ).astype(F32).reshape(1, OWN)
    local_col = jnp.sum(jnp.where(eye, local, 0.0), axis=1, keepdims=True).astype(jnp.int32)
    ones = jnp.ones((16, D), BF16)

    def prep_tile(k0, i, norms, picked):
        k = pl.ds(pl.multiple_of(k0 + i * UNIT, UNIT), UNIT)
        qb = q_ref[k, :]
        qf = qb.astype(F32)
        s2 = qf * qf
        hi = s2.astype(BF16)
        lo = (s2 - hi.astype(F32)).astype(BF16)
        place = lax.broadcasted_iota(jnp.int32, (OWN, UNIT), 1) + (k0 + i * UNIT)
        hot = jnp.where(place == local_col, 1.0, 0.0).astype(BF16)
        for m, part in ((0, hi), (1, lo)):
            pltpu.matmul_push_rhs(part, 0, m, transpose=True)
            pltpu.matmul_acc_lhs(norms[m][i % 2], ones, load_staged_rhs=0)
        pltpu.matmul_push_rhs(qb, 1, i % 2)
        pltpu.matmul_acc_lhs(picked[i % 2], hot, load_staged_rhs=1)
        total = pltpu.matmul_pop(norms[0][i % 2]) + pltpu.matmul_pop(norms[1][i % 2])
        rec_ref[:, k] = lax.rsqrt(total[0:1, :] + EPS)

    def prep(n0, n1, p0, p1):
        size = KQ // PARTS

        def part(p, _):
            queue_copy(p).wait()
            for i in range(size // UNIT):
                prep_tile(p * size, i, (n0, n1), (p0, p1))
            return 0

        lax.fori_loop(0, PARTS, part, 0)
        prow[...] = pltpu.matmul_pop(p0) + pltpu.matmul_pop(p1)

    def two_norms(m):
        return [pltpu.ACC(m)((16, D), F32)] * 2

    pl.run_scoped(prep, two_norms(0), two_norms(1), pltpu.ACC(0)((OWN, D), F32), pltpu.ACC(1)((OWN, D), F32))

    norms_to_partner().start()

    pl.semaphore_wait(go_near, len(NEAR))
    for j in range(KNOWN, 4):
        row_copy(1, j).start()
    for o in COLUMN:
        pl.semaphore_signal(go_column, inc=1, device_id=device(o), device_id_type=MESH)

    def to_owner(t, j):
        i = t * 4 + j
        return remote(sbuf.at[t, pl.ds(j * PC, PC)], abuf.at[i], as_.at[i], ar.at[i], chip(t, j))

    def finish_chunk(t, slot, moments):
        popped = pltpu.matmul_pop(moments)
        for j in range(4):
            src, dst = j * OWN, j * PC
            sbuf[t, dst:dst + OWN, :] = popped[src:src + OWN, :]
            col = jnp.sum(tacc[slot, src:src + OWN, :], axis=1, keepdims=True)
            row = jnp.sum(jnp.where(eye, col, 0.0), axis=0, keepdims=True)
            sbuf[t, dst + OWN:dst + PC, :] = jnp.zeros((8, D), F32)
            sbuf[t, dst + OWN:dst + PC, 0:OWN] = jnp.broadcast_to(row, (8, OWN))

    def chunks(*accumulators):
        scores, moments = accumulators[:NS], accumulators[NS]
        wbuf[...] = jnp.zeros_like(wbuf)
        tacc[...] = jnp.zeros_like(tacc)

        def entries(t, u):
            if u >= 0:
                return pl.ds(u * UNIT, UNIT)
            return pl.ds(pl.multiple_of(lax.min(t, 1) * (UNITS + u) * UNIT, UNIT), UNIT)

        def start_scores(t, u):
            pltpu.matmul_push_rhs(q_ref[entries(t, u), :], u % 2, 0, transpose=True)
            pltpu.matmul_acc_lhs(scores[u % NS], rows[t], load_staged_rhs=u % 2)

        def exponential(t, u):
            slot = lax.rem(t, 2) if u >= 0 else lax.rem(t + 1, 2)
            r = rec_ref[:, entries(t, u)]
            e = jnp.exp2(pltpu.matmul_pop(scores[u % NS]) * (r * (LOG2E * SHARP)))
            tacc[slot] = tacc[slot] + (e[:, 0:128] + e[:, 128:256])
            wbuf[u % NW] = (e * r).astype(BF16)

        def start_moments(t, u):
            pltpu.matmul_push_rhs(q_ref[entries(t, u), :], u % 2, 1)
            pltpu.matmul_acc_lhs(moments, wbuf[u % NW], load_staged_rhs=u % 2)

        def body(t, _):
            for t2 in range(NCH):
                @pl.when(t == t2)
                def _(t2=t2):
                    for j in range(4):
                        if t2 or j:
                            row_copy(t2, j).wait_recv()

            for s in range(UNITS):
                if s == SEND:
                    for t2 in range(NCH - 1):
                        @pl.when(t == t2 + 1)
                        def _(t2=t2):
                            for j in range(4):
                                if t2 or j:
                                    to_owner(t2, j).start()
                if s == SEND_LATER:
                    @pl.when(t == 0)
                    def _():
                        for t2 in (2, 3):
                            for j in range(4):
                                row_copy(t2, j).start()
                if s in QUEUE_WAITS:
                    @pl.when(t == 0)
                    def _(s=s):
                        if s == UNITS // 2:
                            norms_to_partner().wait_recv()
                        for i in QUEUE_WAITS[s]:
                            queue_to_partner(i).wait_recv()
                start_scores(t, s)
                if s == LAG_V:
                    tacc[lax.rem(t, 2)] = jnp.zeros((CH, 128), F32)
                exponential(t, s - LAG_V)
                start_moments(t, s - LAG_M)
                if s == LAG_M - 1:
                    finish_chunk(lax.max(t - 1, 0), lax.rem(t + 1, 2), moments)
            return 0

        lax.fori_loop(0, NCH, body, 0)
        last = NCH - 1
        for s in range(UNITS, UNITS + LAG_M):
            if s - LAG_V < UNITS:
                exponential(last, s - LAG_V)
            start_moments(last, s - LAG_M)
        finish_chunk(last, last % 2, moments)
        for j in range(4):
            to_owner(last, j).start()

    pl.run_scoped(chunks, *[pltpu.ACC(0)((UNIT, D), F32)] * NS, pltpu.ACC(1)((UNIT, D), F32))
    pl.semaphore_wait(go_column, len(COLUMN))
    prows = prow[...]
    pushed_away = inverse_norms(prows) * prows
    cot = jnp.sum(jnp.where(eye, cot_ref[...].reshape(1, OWN), 0.0), axis=1, keepdims=True)
    own = sbuf[0, 0:PC, :]
    for i in range(1, 16):
        to_owner(i // 4, i % 4).wait_recv()
        own = own + abuf[i]
    totals = jnp.sum(jnp.where(eye, own[OWN:OWN + 1, 0:OWN], 0.0), axis=1, keepdims=True)
    pushed = own[0:OWN, :] / totals - pushed_away
    tangent = pushed - dirs * jnp.sum(dirs * pushed, axis=1, keepdims=True)
    gradient = cot * tangent * inv

    squares = jnp.sum(gradient * gradient, axis=0, keepdims=True)
    sq[0] = squares[:, 0:128] + squares[:, 128:256]
    for i, o in enumerate(ALL):
        remote(sq.at[0], sq.at[i + 1], ss, sr, device(o)).start()
    others = sq.at[pl.ds(1, len(ALL))]
    remote(others, others, ss, sr, device((0, 0, 1, 0))).wait()
    squares = jnp.sum(jnp.sum(sq[...], axis=0), axis=1, keepdims=True)
    clip_total = OWN * lax.axis_size("bank") * lax.axis_size("dp")
    factor = jnp.minimum(1.0, (4.0 * math.sqrt(clip_total)) / jnp.sqrt(squares + EPS))
    out_ref[...] = gradient * factor

    for i in range(1, 16):
        row_copy(i // 4, i % 4).wait_send()
        to_owner(i // 4, i % 4).wait_send()
    for i in range(PARTS):
        queue_to_partner(i).wait_send()
    norms_to_partner().wait_send()


def shards(clips, queue, positive, cotangent):
    vmem = pl.BlockSpec(memory_space=pltpu.VMEM)
    dma = pltpu.SemaphoreType.DMA
    return pl.pallas_call(
        kernel,
        out_shape=pltpu.VMEM((OWN, D), F32),
        in_specs=[pl.BlockSpec(memory_space=pl.ANY)] * 4,
        out_specs=vmem,
        scratch_shapes=[
            pltpu.VMEM((OWN, D), BF16),
            pltpu.VMEM((OWN,), jnp.int32),
            pltpu.VMEM((OWN,), F32),
            pltpu.VMEM((2 * KQ, D), BF16),
            pltpu.VMEM((1, 2 * KQ), F32),
            pltpu.VMEM((NCH, CH, D), BF16),
            pltpu.VMEM((NW, UNIT, UNIT), BF16),
            pltpu.VMEM((2, CH, 128), F32),
            pltpu.VMEM((NCH, 4 * PC, D), F32),
            pltpu.VMEM((16, PC, D), F32),
            pltpu.VMEM((OWN, D), F32),
            pltpu.VMEM((len(ALL) + 1, 1, 128), F32),
            dma((3,)),
            dma((PARTS,)),
            pltpu.SemaphoreType.REGULAR, pltpu.SemaphoreType.REGULAR,
            dma((PARTS,)), dma((PARTS,)),
            dma, dma,
            dma((16,)), dma((16,)),
            dma((16,)), dma((16,)),
            dma, dma,
        ],
        compiler_params=pltpu.CompilerParams(
            collective_id=0, has_side_effects=True, vmem_limit_bytes=56 << 20),
        cost_estimate=pl.CostEstimate(flops=17 * 10**9, bytes_accessed=5 * 10**6, transcendentals=17 * 10**6),
    )(clips, queue, positive, cotangent)


def solution(mesh):
    in_specs = (P(("bank", "dp"), None), P("bank", None), P(("bank", "dp")), P(("bank", "dp")))
    return jax.shard_map(shards, mesh=mesh, in_specs=in_specs, out_specs=P(("bank", "dp"), None), check_vma=False)
```
